32 devices in a mesh: dp: 8 (over y, x, core), feat: 4 (over z).
Axes of the slice: x: 2, y: 2, z: 4, core: 2. Of those that a mesh axis runs over, the one named last changes fastest.
Arguments:
- tokens: bfloat16 [1024, 8192], P('dp', 'feat'), may hold values from -6 to 6
- targets: bfloat16 [2048, 8192], P('dp', 'feat'), may hold values from -6 to 6
- first_blocks: bfloat16 [128, 64, 256], P('feat'), may hold values from -0.75 to 0.75
- second_factor_blocks: bfloat16 [128, 256, 256], P('feat'), may hold values from -0.375 to 0.375
- down_blocks: bfloat16 [128, 256, 64], P('feat'), may hold values from -0.375 to 0.375
- first_tangent: bfloat16 [128, 64, 256], P('feat'), may hold values from -0.75 to 0.75
- second_factor_tangent: bfloat16 [128, 256, 256], P('feat'), may hold values from -0.375 to 0.375
- doc_lengths: int32 [8, 8], replicated, may hold values from 1 to 32, as said below
- doc_owners: int32 [8, 8], replicated, may hold values from 0 to 7, as said below
- pack_offsets: int32 [8, 8], replicated, may hold values from 0 to 224, as said below
Outputs:
- hess_first: float32 [128, 64, 256], P('feat', 'dp')
- hess_mixed: float32 [128, 256, 256], P('feat', 'dp')
The draws below stay inside these ranges and needn't reach their ends.
Inputs may be any that keep to these rules, and one draw needn't show every extreme that they name: `doc_lengths`: the 8 lengths of one loader sum to 128; the longest has exactly 32 rows. `doc_owners`: A loader sends exactly one document to each owner; some owner receives exactly 256 rows in all, and none more. `pack_offsets`: each owner's documents lie end to end from row 0 of its pack, in the order of their loaders.
All inputs are finite; a program needn't handle non-finite values.
Results may differ from the reference program's by a relative error of at most 0.0072.
Values may be sent and summed in bfloat16 or wider, within the bound.
A program may use at most 128 MiB of HBM per device.

```python
import jax
import jax.numpy as jnp
from jax import lax

D = 8192
NB = 128
BS = 256
TOK_DEV = 128
IN_B = 64
CM = 2
DOCS_DEV = 8
MOST = 32
OWN_CAP = 256
TOKENS = 1024
N_DP = 8


def doc_tables(key):
    loaders = N_DP
    docs = DOCS_DEV
    longest = MOST
    rank_owner = jax.random.permutation(jax.random.fold_in(key, 11), loaders).astype(jnp.int32)
    rank_loader = jax.random.permutation(jax.random.fold_in(key, 12), loaders).astype(jnp.int32)
    columns = jnp.arange(docs, dtype=jnp.int32)
    circle = (rank_loader[:, None] + columns[None, :]) % loaders
    owners = rank_owner[circle]
    long_col = (loaders - rank_loader) % loaders
    is_long = columns[None, :] == long_col[:, None]
    shares = jax.random.randint(jax.random.fold_in(key, 14), (loaders, docs), 4, 8, dtype=jnp.int32)
    shares = jnp.where(is_long, 0, shares)
    extra = TOK_DEV - longest - (docs - 1)
    share_total = jnp.sum(shares, axis=1, keepdims=True)
    portion = extra * shares // share_total
    leftover = extra - jnp.sum(portion, axis=1, keepdims=True)
    order_rank = jnp.cumsum(jnp.logical_not(is_long).astype(jnp.int32), axis=1) - 1
    lengths = jnp.where(is_long, longest, 1 + portion + (order_rank < leftover).astype(jnp.int32))
    matched = (owners[:, :, None] == jnp.arange(loaders, dtype=jnp.int32)[None, None, :]).astype(jnp.int32)
    owner_load = jnp.sum(matched * lengths[:, :, None], axis=1)
    before = jnp.cumsum(owner_load, axis=0) - owner_load
    offsets = jnp.sum(matched * before[:, None, :], axis=2)
    return (lengths.astype(jnp.int32), owners.astype(jnp.int32), offsets.astype(jnp.int32))


def draw_doc_lengths(key, part):
    return doc_tables(key)[0]


def draw_doc_owners(key, part):
    return doc_tables(key)[1]


def draw_pack_offsets(key, part):
    return doc_tables(key)[2]


def level_of(key, shape, pieces, least, high):
    def one(dim, blocks):
        draws = jax.random.uniform(jax.random.fold_in(jax.random.fold_in(key, 6), dim), (blocks,), jnp.float32, least / len(pieces), high / len(pieces))
        return jnp.repeat(jnp.exp(draws), shape[dim] // blocks).reshape((-1,) + (1,) * (len(shape) - dim - 1))

    factor_of = one(*pieces[0])
    for cut in pieces[1:]:
        factor_of = factor_of * one(*cut)
    return factor_of


def noise(stream_key, dims, scale, bound, shards=(), kind=jnp.bfloat16):
    gain = level_of(stream_key, dims, shards, -0.22, 0.18) if shards else 1.0
    array = jax.random.normal(stream_key, dims, jnp.float32) * scale * gain
    return jnp.minimum(jnp.maximum(array, -bound), bound).astype(kind)


def setup_inputs(seed: int = 0) -> dict:
    streams_of = jax.random.split(jax.random.key(seed), 11)
    return {
        "tokens": noise(streams_of[0], (TOKENS, D), 1.0, 6.0, ((0, 8), (1, 4))),
        "targets": noise(streams_of[1], (N_DP * OWN_CAP, D), 1.0, 6.0, ((0, 8), (1, 4))),
        "first_blocks": noise(streams_of[2], (NB, D // NB, BS), (D // NB) ** -0.5, 0.75, ((0, 4),)),
        "second_factor_blocks": noise(streams_of[3], (NB, BS, BS), BS ** -0.5, 0.375, ((0, 4),)),
        "down_blocks": noise(streams_of[4], (NB, BS, D // NB), BS ** -0.5, 0.375, ((0, 4),)),
        "first_tangent": noise(streams_of[5], (NB, D // NB, BS), (D // NB) ** -0.5, 0.75, ((0, 4),)),
        "second_factor_tangent": noise(streams_of[6], (NB, BS, BS), BS ** -0.5, 0.375, ((0, 4),)),
        "doc_lengths": draw_doc_lengths(jax.random.fold_in(streams_of[10], 71), 0),
        "doc_owners": draw_doc_owners(jax.random.fold_in(streams_of[10], 71), 0),
        "pack_offsets": draw_pack_offsets(jax.random.fold_in(streams_of[10], 71), 0),
    }


inv_root_two = 0.7071067811865476
inv_root_two_pi = 0.3989422804014327


def permute_blocks(values):
    row_count = values.shape[0]
    return values.reshape(row_count, NB, NB, CM).transpose(0, 2, 1, 3).reshape(row_count, NB, BS)


def round_wide(values):
    return lax.optimization_barrier(values.astype(jnp.bfloat16)).astype(jnp.float32)


def reference(tokens, targets, first_blocks, second_factor_blocks, down_blocks, first_tangent, second_factor_tangent, doc_lengths, doc_owners, pack_offsets):
    first_full = first_blocks.astype(jnp.float32)
    mixed_full = second_factor_blocks.astype(jnp.float32)
    down_full = down_blocks.astype(jnp.float32)
    first_tan_full = first_tangent.astype(jnp.float32)
    mixed_tan_full = second_factor_tangent.astype(jnp.float32)
    position = jnp.arange(TOK_DEV, dtype=jnp.int32)

    def one_loader(carry, loader):
        hess_first, hess_mixed = carry
        tok_rows = lax.dynamic_slice_in_dim(tokens, loader * TOK_DEV, TOK_DEV, 0)
        lengths = doc_lengths[loader]
        owners = doc_owners[loader]
        offsets = pack_offsets[loader]
        starts = jnp.cumsum(lengths) - lengths
        inside = (position[:, None] >= starts[None, :]) & (position[:, None] < (starts + lengths)[None, :])
        inside_int = inside.astype(jnp.int32)
        goal_index = jnp.sum(inside_int * (owners * OWN_CAP + offsets - starts)[None, :], axis=1) + position
        weight = jnp.sum(inside.astype(jnp.float32) / lengths.astype(jnp.float32)[None, :], axis=1)
        goal_rows = jnp.take(targets, goal_index.astype(jnp.int32), axis=0)
        token_blocks = tok_rows.astype(jnp.float32).reshape(TOK_DEV, NB, IN_B)
        goal_blocks = goal_rows.astype(jnp.float32).reshape(TOK_DEV, NB, IN_B)
        first_act = round_wide(jnp.einsum("tki,kij->tkj", token_blocks, first_full))
        tan_act = round_wide(jnp.einsum("tki,kij->tkj", token_blocks, first_tan_full))
        out_grad = round_wide(jnp.einsum("tkd,kmd->tkm", goal_blocks, down_full) * weight[:, None, None])
        mixed_activation = permute_blocks(first_act)
        mixed_tangent_value = permute_blocks(tan_act)
        hidden_grad = permute_blocks(out_grad)
        pre_act = jnp.einsum("tgm,gmj->tgj", mixed_activation, mixed_full)
        pre_tan = jnp.einsum("tgm,gmj->tgj", mixed_tangent_value, mixed_full) + jnp.einsum("tgm,gmj->tgj", mixed_activation, mixed_tan_full)
        density = jnp.exp(-0.5 * pre_act * pre_act) * inv_root_two_pi
        normal_cdf = 0.5 * (1.0 + lax.erf(pre_act * inv_root_two))
        preactivation_gradient = round_wide(hidden_grad * (normal_cdf + pre_act * density))
        preactivation_tangent_gradient = round_wide(hidden_grad * (density * (2.0 - pre_act * pre_act)) * pre_tan)
        hess_mixed = hess_mixed + jnp.einsum("tgm,tgj->gmj", mixed_tangent_value, preactivation_gradient) + jnp.einsum("tgm,tgj->gmj", mixed_activation, preactivation_tangent_gradient)
        back_mixed = round_wide(jnp.einsum("tgj,gmj->tgm", preactivation_tangent_gradient, mixed_full) + jnp.einsum("tgj,gmj->tgm", preactivation_gradient, mixed_tan_full))
        back_first = permute_blocks(back_mixed)
        hess_first = hess_first + jnp.einsum("tki,tkj->kij", token_blocks, back_first)
        return (hess_first, hess_mixed), None

    first_factor_start = jnp.zeros((NB, IN_B, BS), jnp.float32)
    start_mixed = jnp.zeros((NB, BS, BS), jnp.float32)
    (hess_first, hess_mixed), _ = lax.scan(one_loader, (first_factor_start, start_mixed), jnp.arange(N_DP, dtype=jnp.int32))
    return hess_first, hess_mixed
```

```python
import jax
import jax.numpy as jnp
from jax import lax
from jax.experimental import pallas as pl
from jax.experimental.pallas import tpu as pltpu
from jax.sharding import PartitionSpec as P

inv_root_two = 0.7071067811865476
inv_root_two_pi = 0.3989422804014327
STEP = 2


def mixed_kernel(act_ref, tan_ref, grad_ref, fac_ref, fac_tan_ref, hess_ref, back_ref):
    rows = act_ref.shape[2]
    for b in range(act_ref.shape[0]):
        act = act_ref[b]
        tan = tan_ref[b]
        fac = fac_ref[b]
        fac_tan = fac_tan_ref[b]
        first_dims = (((0,), (0,)), ((), ()))
        both = lax.dot_general(
            fac,
            jnp.concatenate([act, tan], axis=1),
            first_dims,
            preferred_element_type=jnp.float32,
        )
        pre_act = both[:, :rows]
        pre_tan = both[:, rows:] + lax.dot_general(
            fac_tan, act, first_dims, preferred_element_type=jnp.float32
        )
        grad = grad_ref[b].astype(jnp.float32)
        density = jnp.exp(-0.5 * pre_act * pre_act) * inv_root_two_pi
        cdf = 0.5 * (1.0 + lax.erf(pre_act * inv_root_two))
        pre_grad = (grad * (cdf + pre_act * density)).astype(jnp.bfloat16)
        pre_tan_grad = (grad * (density * (2.0 - pre_act * pre_act)) * pre_tan).astype(
            jnp.bfloat16
        )
        hess_ref[b] = lax.dot_general(
            jnp.concatenate([tan, act], axis=1),
            jnp.concatenate([pre_grad, pre_tan_grad], axis=1),
            (((1,), (1,)), ((), ())),
            preferred_element_type=jnp.float32,
        ).astype(hess_ref.dtype)
        back_ref[b] = (
            jnp.dot(fac, pre_tan_grad, preferred_element_type=jnp.float32)
            + jnp.dot(fac_tan, pre_grad, preferred_element_type=jnp.float32)
        ).astype(back_ref.dtype)


def mixed_stage(act, tan, grad, fac, fac_tan):
    blocks, width, rows = act.shape
    thin = pl.BlockSpec((STEP, width, rows), lambda s: (s, 0, 0))
    wide = pl.BlockSpec((STEP, width, width), lambda s: (s, 0, 0))
    return pl.pallas_call(
        mixed_kernel,
        grid=(blocks // STEP,),
        in_specs=[thin, thin, thin, wide, wide],
        out_specs=[wide, thin],
        out_shape=[
            jax.ShapeDtypeStruct((blocks, width, width), jnp.bfloat16),
            jax.ShapeDtypeStruct((blocks, width, rows), jnp.bfloat16),
        ],
        compiler_params=pltpu.CompilerParams(vmem_limit_bytes=32 * 1024 * 1024),
        cost_estimate=pl.CostEstimate(
            flops=14 * blocks * width * width * rows,
            bytes_accessed=blocks * width * (6 * width + 8 * rows),
            transcendentals=2 * blocks * width * rows,
        ),
    )(act, tan, grad, fac, fac_tan)


def per_device(
    tokens,
    targets,
    first_blocks,
    second_factor_blocks,
    down_blocks,
    first_tangent,
    second_factor_tangent,
    doc_lengths,
    doc_owners,
    pack_offsets,
):
    loaders = lax.axis_size("dp")
    features = lax.axis_size("feat")
    device = lax.axis_index("dp")
    tok_count, feature_cols = tokens.shape
    pack_rows = targets.shape[0]
    slot_rows = 2 * tok_count // loaders
    local_blocks, block_in, block_out = first_blocks.shape
    all_blocks = local_blocks * features
    local_out = block_out // features
    pair = local_out // local_blocks

    position = jnp.arange(slot_rows, dtype=jnp.int32)
    mine = (doc_owners == device).astype(jnp.int32)
    slot_start = jnp.sum(mine * pack_offsets, axis=1)
    pack_source = jnp.minimum(slot_start[:, None] + position[None, :], pack_rows - 1)
    outgoing = jnp.take(targets, pack_source.reshape(-1), axis=0).reshape(
        loaders, slot_rows, feature_cols
    )
    arrived = lax.all_to_all(outgoing, "dp", split_axis=0, concat_axis=0, tiled=True)
    my_lengths = lax.dynamic_index_in_dim(doc_lengths, device, 0, keepdims=False)
    my_owners = lax.dynamic_index_in_dim(doc_owners, device, 0, keepdims=False)
    my_starts = jnp.cumsum(my_lengths) - my_lengths
    row = jnp.arange(tok_count, dtype=jnp.int32)
    inside = (row[:, None] >= my_starts[None, :]) & (
        row[:, None] < (my_starts + my_lengths)[None, :]
    )
    inside_int = inside.astype(jnp.int32)
    source = jnp.sum(inside_int * (my_owners * slot_rows - my_starts)[None, :], axis=1) + row
    weight = jnp.sum(inside.astype(jnp.float32) / my_lengths.astype(jnp.float32)[None, :], axis=1)
    goal = jnp.take(arrived.reshape(loaders * slot_rows, feature_cols), source, axis=0)

    rows = local_blocks * block_in
    share = rows // loaders
    factors = jnp.stack(
        [
            lax.dynamic_slice_in_dim(w.reshape(rows, block_out), device * share, share, 0)
            for w in (first_blocks, first_tangent, jnp.swapaxes(down_blocks, 1, 2))
        ]
    )
    factors = factors.reshape(3, share, features, local_out).transpose(2, 0, 3, 1)
    factors = lax.all_to_all(factors, "feat", split_axis=0, concat_axis=0, tiled=True)
    factors = lax.all_gather(factors, "dp", axis=0, tiled=False)
    factors = factors.transpose(2, 3, 1, 0, 4).reshape(3, local_out, all_blocks, block_in)

    tok_all = lax.all_gather(tokens, "feat", axis=0, tiled=False)
    tok_all = tok_all.transpose(0, 2, 1).reshape(all_blocks, block_in, tok_count)
    goal_all = lax.all_gather(goal, "feat", axis=0, tiled=False)
    goal_all = goal_all.transpose(0, 2, 1).reshape(all_blocks, block_in, tok_count)

    def mix(values):
        return (
            values.astype(jnp.bfloat16)
            .reshape(all_blocks, local_blocks, pair, tok_count)
            .transpose(1, 0, 2, 3)
            .reshape(local_blocks, block_out, tok_count)
        )

    def first(weights, rows_of):
        return jnp.einsum("jki,kir->kjr", weights, rows_of, preferred_element_type=jnp.float32)

    act = mix(first(factors[0], tok_all))
    tan = mix(first(factors[1], tok_all))
    grad = mix(first(factors[2], goal_all) * weight)
    hess_mixed, back = mixed_stage(act, tan, grad, second_factor_blocks, second_factor_tangent)
    hess_mixed = lax.psum_scatter(hess_mixed, "dp", scatter_dimension=1, tiled=True)

    back = (
        back.reshape(local_blocks, all_blocks, pair, tok_count)
        .transpose(1, 0, 2, 3)
        .reshape(all_blocks, local_out, tok_count)
    )
    hess_first = jnp.einsum("kjr,kir->kij", back, tok_all, preferred_element_type=jnp.float32)
    in_share = block_in // loaders
    hess_first = hess_first.astype(jnp.bfloat16).reshape(
        all_blocks, loaders, in_share * local_out
    )
    hess_first = lax.psum_scatter(
        hess_first.transpose(1, 0, 2), "dp", scatter_dimension=0, tiled=True
    )
    hess_first = hess_first.reshape(features, local_blocks, in_share * local_out)
    hess_first = lax.all_to_all(hess_first, "feat", split_axis=0, concat_axis=0, tiled=True)
    hess_first = (
        hess_first.reshape(features, local_blocks, in_share, local_out)
        .transpose(1, 2, 0, 3)
        .reshape(local_blocks, in_share, block_out)
    )
    return hess_first.astype(jnp.float32), hess_mixed.astype(jnp.float32)


def solution(mesh):
    in_specs = (
        P("dp", "feat"),
        P("dp", "feat"),
        P("feat", None, None),
        P("feat", None, None),
        P("feat", None, None),
        P("feat", None, None),
        P("feat", None, None),
        P(),
        P(),
        P(),
    )
    out_specs = (P("feat", "dp", None), P("feat", "dp", None))
    return jax.shard_map(
        per_device, mesh=mesh, in_specs=in_specs, out_specs=out_specs, check_vma=False
    )
```

```python
import functools

import jax
import jax.numpy as jnp
from jax import lax
from jax.experimental import pallas as pl
from jax.experimental.pallas import tpu as pltpu
from jax.sharding import PartitionSpec as P

inv_root_two = 0.7071067811865476
inv_root_two_pi = 0.3989422804014327
STEP = 2
MESH = pl.DeviceIdType.MESH


def column_loop(columns, body):
    tile = min(columns, 256)

    @pl.loop(0, columns // tile)
    def _(step):
        body(pl.ds(pl.multiple_of(step * tile, tile), tile))


def gather_kernel(
    loaders,
    features,
    tok_ref,
    target_ref,
    send_sel_ref,
    take_sel_ref,
    fac_ref,
    tok_all,
    goal_all,
    fac_all,
    outgoing,
    arrived,
    slot_send,
    slot_recv,
    fac_send,
    fac_recv,
    chip_send,
    chip_recv,
    pair_send,
    pair_recv,
    line_send,
    line_recv,
):
    dev = lax.axis_index("dp")
    me = lax.axis_index("feat")
    columns = tok_ref.shape[1]
    slot = outgoing.shape[0] // loaders

    def to_dp(peer):
        return {"dp": peer}

    def to_feat(peer):
        return {"feat": peer}

    barrier = pltpu.get_barrier_semaphore()
    for off in range(1, loaders):
        pl.semaphore_signal(
            barrier, inc=1, device_id=to_dp(lax.rem(dev + off, loaders)), device_id_type=MESH
        )
    for off in range(1, features):
        pl.semaphore_signal(
            barrier, inc=1, device_id=to_feat(lax.rem(me + off, features)), device_id_type=MESH
        )
    pl.semaphore_wait(barrier, loaders + features - 2)

    def remote(src, dst, send, recv, target):
        return pltpu.make_async_remote_copy(
            src_ref=src,
            dst_ref=dst,
            send_sem=send,
            recv_sem=recv,
            device_id=target,
            device_id_type=MESH,
        )

    fac_copies = []
    for off in range(1, features):
        peer = lax.rem(me + off, features)
        fac_copies.append(
            remote(
                fac_ref.at[peer],
                fac_all.at[dev, me],
                fac_send.at[off - 1],
                fac_recv.at[off - 1],
                to_feat(peer),
            )
        )
        fac_copies[-1].start()
    fac_all[dev, me] = fac_ref[me]

    def hop(ref, which, step, right):
        shard = jnp.maximum(me - step, 0) if right else jnp.minimum(me + step, features - 1)
        peer = jnp.minimum(me + 1, features - 1) if right else jnp.maximum(me - 1, 0)
        side = 0 if right else 1
        return remote(
            ref.at[shard],
            ref.at[shard],
            line_send.at[which, side, step],
            line_recv.at[which, side, step],
            to_feat(peer),
        )

    def has(step, right):
        return (me >= step) if right else (me + step <= features - 1)

    def sends(step, right):
        return has(step, right) & ((me < features - 1) if right else (me > 0))

    def line_step(ref, which, step):
        for right in (True, False):
            if step > 0:

                @pl.when(has(step, right))
                def _():
                    hop(ref, which, step - 1, right).wait_recv()

            if step < features - 1:

                @pl.when(sends(step, right))
                def _():
                    hop(ref, which, step, right).start()

    def line_end(ref, which):
        for step in range(features - 1):
            for right in (True, False):

                @pl.when(sends(step, right))
                def _():
                    hop(ref, which, step, right).wait_send()

    def turn_tokens(cols):
        tok_all[me, cols, :] = tok_ref[:, cols].T

    column_loop(columns, turn_tokens)
    line_step(tok_all, 0, 0)

    def pick(cols):
        outgoing[:, cols] = jnp.dot(
            send_sel_ref[...], target_ref[:, cols], preferred_element_type=jnp.float32
        ).astype(jnp.bfloat16)

    column_loop(columns, pick)
    slot_copies = []
    for off in range(1, loaders):
        peer = lax.rem(dev + off, loaders)
        slot_copies.append(
            remote(
                outgoing.at[pl.ds(pl.multiple_of(peer * slot, slot), slot)],
                arrived.at[pl.ds(pl.multiple_of(dev * slot, slot), slot)],
                slot_send.at[off - 1],
                slot_recv.at[off - 1],
                to_dp(peer),
            )
        )
        slot_copies[-1].start()
    own = pl.ds(pl.multiple_of(dev * slot, slot), slot)
    arrived[own] = outgoing[own]

    for copy in fac_copies:
        copy.wait_recv()
    chips = loaders // 2
    chip = dev // 2
    core = lax.rem(dev, 2)
    sibling = dev + 1 - 2 * core

    def to_pair(index, piece):
        return remote(
            fac_all.at[piece],
            fac_all.at[piece],
            pair_send.at[index],
            pair_recv.at[index],
            to_dp(sibling),
        )

    pair_copies = [to_pair(0, dev)]
    pair_copies[0].start()
    chip_copies = []
    for off in range(1, chips):
        peer = lax.rem(chip + off, chips) * 2 + core
        chip_copies.append(
            remote(
                fac_all.at[dev],
                fac_all.at[dev],
                chip_send.at[off - 1],
                chip_recv.at[off - 1],
                to_dp(peer),
            )
        )
        chip_copies[-1].start()

    if features > 2:
        line_step(tok_all, 0, 1)
    for copy in slot_copies:
        copy.wait_recv()

    def take(cols):
        goal_all[me, cols, :] = lax.dot_general(
            arrived[:, cols],
            take_sel_ref[...],
            (((0,), (0,)), ((), ())),
            preferred_element_type=jnp.float32,
        ).astype(jnp.bfloat16)

    column_loop(columns, take)
    line_step(goal_all, 1, 0)
    for step in range(2, features):
        line_step(tok_all, 0, step)
    for off in range(1, chips):
        chip_copies[off - 1].wait_recv()
        piece = lax.rem(chip + chips - off, chips) * 2 + core
        pair_copies.append(to_pair(off, piece))
        pair_copies[-1].start()
    for step in range(1, features):
        line_step(goal_all, 1, step)
    for copy in pair_copies:
        copy.wait()
    for copy in slot_copies + fac_copies + chip_copies:
        copy.wait_send()
    line_end(tok_all, 0)
    line_end(goal_all, 1)


def gather_stage(loaders, features, tokens, targets, send_sel, take_sel, factors):
    rows, columns = tokens.shape
    slots = send_sel.shape[0]
    dma = pltpu.SemaphoreType.DMA
    vmem = pl.BlockSpec(memory_space=pltpu.VMEM)
    return pl.pallas_call(
        functools.partial(gather_kernel, loaders, features),
        in_specs=[vmem] * 5,
        out_specs=[vmem] * 3,
        out_shape=[
            jax.ShapeDtypeStruct((features, columns, rows), jnp.bfloat16),
            jax.ShapeDtypeStruct((features, columns, rows), jnp.bfloat16),
            jax.ShapeDtypeStruct((loaders,) + factors.shape, jnp.bfloat16),
        ],
        scratch_shapes=[
            pltpu.VMEM((slots, columns), jnp.bfloat16),
            pltpu.VMEM((slots, columns), jnp.bfloat16),
            dma((loaders - 1,)),
            dma((loaders - 1,)),
            dma((features - 1,)),
            dma((features - 1,)),
            dma((loaders // 2 - 1,)),
            dma((loaders // 2 - 1,)),
            dma((loaders // 2,)),
            dma((loaders // 2,)),
            dma((2, 2, features - 1)),
            dma((2, 2, features - 1)),
        ],
        compiler_params=pltpu.CompilerParams(
            collective_id=0, has_side_effects=True, vmem_limit_bytes=48 * 1024 * 1024
        ),
    )(tokens, targets, send_sel, take_sel, factors)


def mixed_kernel(act_ref, tan_ref, grad_ref, fac_ref, fac_tan_ref, hess_ref, back_ref):
    rows = act_ref.shape[2]
    for b in range(act_ref.shape[0]):
        act = act_ref[b]
        tan = tan_ref[b]
        fac = fac_ref[b]
        fac_tan = fac_tan_ref[b]
        first_dims = (((0,), (0,)), ((), ()))
        both = lax.dot_general(
            fac,
            jnp.concatenate([act, tan], axis=1),
            first_dims,
            preferred_element_type=jnp.float32,
        )
        pre_act = both[:, :rows]
        pre_tan = both[:, rows:] + lax.dot_general(
            fac_tan, act, first_dims, preferred_element_type=jnp.float32
        )
        grad = grad_ref[b].astype(jnp.float32)
        density = jnp.exp(-0.5 * pre_act * pre_act) * inv_root_two_pi
        cdf = 0.5 * (1.0 + lax.erf(pre_act * inv_root_two))
        pre_grad = (grad * (cdf + pre_act * density)).astype(jnp.bfloat16)
        pre_tan_grad = (grad * (density * (2.0 - pre_act * pre_act)) * pre_tan).astype(
            jnp.bfloat16
        )
        hess_ref[b] = lax.dot_general(
            jnp.concatenate([tan, act], axis=1),
            jnp.concatenate([pre_grad, pre_tan_grad], axis=1),
            (((1,), (1,)), ((), ())),
            preferred_element_type=jnp.float32,
        ).astype(hess_ref.dtype)
        back_ref[b] = (
            jnp.dot(fac, pre_tan_grad, preferred_element_type=jnp.float32)
            + jnp.dot(fac_tan, pre_grad, preferred_element_type=jnp.float32)
        ).astype(back_ref.dtype)


def mixed_stage(act, tan, grad, fac, fac_tan):
    blocks, width, rows = act.shape
    thin = pl.BlockSpec((STEP, width, rows), lambda s: (s, 0, 0))
    wide = pl.BlockSpec((STEP, width, width), lambda s: (s, 0, 0))
    return pl.pallas_call(
        mixed_kernel,
        grid=(blocks // STEP,),
        in_specs=[thin, thin, thin, wide, wide],
        out_specs=[wide, thin],
        out_shape=[
            jax.ShapeDtypeStruct((blocks, width, width), jnp.bfloat16),
            jax.ShapeDtypeStruct((blocks, width, rows), jnp.bfloat16),
        ],
        compiler_params=pltpu.CompilerParams(vmem_limit_bytes=32 * 1024 * 1024),
        cost_estimate=pl.CostEstimate(
            flops=14 * blocks * width * width * rows,
            bytes_accessed=blocks * width * (6 * width + 8 * rows),
            transcendentals=2 * blocks * width * rows,
        ),
    )(act, tan, grad, fac, fac_tan)


def per_device(
    tokens,
    targets,
    first_blocks,
    second_factor_blocks,
    down_blocks,
    first_tangent,
    second_factor_tangent,
    doc_lengths,
    doc_owners,
    pack_offsets,
):
    loaders = lax.axis_size("dp")
    features = lax.axis_size("feat")
    device = lax.axis_index("dp")
    tok_count, feature_cols = tokens.shape
    pack_rows = targets.shape[0]
    slot_rows = -(-2 * tok_count // (16 * loaders)) * 16
    local_blocks, block_in, block_out = first_blocks.shape
    all_blocks = local_blocks * features
    local_out = block_out // features
    pair = local_out // local_blocks

    position = jnp.arange(slot_rows, dtype=jnp.int32)
    mine = (doc_owners == device).astype(jnp.int32)
    slot_start = jnp.sum(mine * pack_offsets, axis=1)
    pack_source = (slot_start[:, None] + position[None, :]).reshape(-1)
    send_sel = (
        pack_source[:, None] == jnp.arange(pack_rows, dtype=jnp.int32)[None, :]
    ).astype(jnp.bfloat16)
    my_lengths = lax.dynamic_index_in_dim(doc_lengths, device, 0, keepdims=False)
    my_owners = lax.dynamic_index_in_dim(doc_owners, device, 0, keepdims=False)
    my_starts = jnp.cumsum(my_lengths) - my_lengths
    row = jnp.arange(tok_count, dtype=jnp.int32)
    inside = (row[:, None] >= my_starts[None, :]) & (
        row[:, None] < (my_starts + my_lengths)[None, :]
    )
    inside_int = inside.astype(jnp.int32)
    source = jnp.sum(inside_int * (my_owners * slot_rows - my_starts)[None, :], axis=1) + row
    weight = jnp.sum(inside.astype(jnp.float32) / my_lengths.astype(jnp.float32)[None, :], axis=1)
    take_sel = (
        jnp.arange(loaders * slot_rows, dtype=jnp.int32)[:, None] == source[None, :]
    ).astype(jnp.bfloat16)

    rows = local_blocks * block_in
    share = rows // loaders
    factors = jnp.stack(
        [
            lax.dynamic_slice_in_dim(w.reshape(rows, block_out), device * share, share, 0)
            for w in (first_blocks, first_tangent, jnp.swapaxes(down_blocks, 1, 2))
        ]
    )
    factors = factors.reshape(3, share, features, local_out).transpose(2, 0, 3, 1)
    factors = factors.reshape(features, 3 * local_out, share)
    tok_all, goal_all, factors = gather_stage(
        loaders, features, tokens, targets, send_sel, take_sel, factors
    )
    factors = factors.reshape(loaders, features, 3, local_out, share)
    factors = factors.transpose(2, 3, 1, 0, 4).reshape(3, local_out, all_blocks, block_in)
    tok_all = tok_all.reshape(all_blocks, block_in, tok_count)
    goal_all = goal_all.reshape(all_blocks, block_in, tok_count)

    def mix(values):
        return (
            values.astype(jnp.bfloat16)
            .reshape(all_blocks, local_blocks, pair, tok_count)
            .transpose(1, 0, 2, 3)
            .reshape(local_blocks, block_out, tok_count)
        )

    def first(weights, rows_of):
        return jnp.einsum("jki,kir->kjr", weights, rows_of, preferred_element_type=jnp.float32)

    act = mix(first(factors[0], tok_all))
    tan = mix(first(factors[1], tok_all))
    grad = mix(first(factors[2], goal_all) * weight)
    hess_mixed, back = mixed_stage(act, tan, grad, second_factor_blocks, second_factor_tangent)
    hess_mixed = lax.psum_scatter(hess_mixed, "dp", scatter_dimension=1, tiled=True)

    back = (
        back.reshape(local_blocks, all_blocks, pair, tok_count)
        .transpose(1, 0, 2, 3)
        .reshape(all_blocks, local_out, tok_count)
    )
    hess_first = jnp.einsum("kjr,kir->kij", back, tok_all, preferred_element_type=jnp.float32)
    in_share = block_in // loaders
    hess_first = hess_first.astype(jnp.bfloat16).reshape(
        all_blocks, loaders, in_share * local_out
    )
    hess_first = lax.psum_scatter(
        hess_first.transpose(1, 0, 2), "dp", scatter_dimension=0, tiled=True
    )
    hess_first = hess_first.reshape(features, local_blocks, in_share * local_out)
    hess_first = lax.all_to_all(hess_first, "feat", split_axis=0, concat_axis=0, tiled=True)
    hess_first = (
        hess_first.reshape(features, local_blocks, in_share, local_out)
        .transpose(1, 2, 0, 3)
        .reshape(local_blocks, in_share, block_out)
    )
    return hess_first.astype(jnp.float32), hess_mixed.astype(jnp.float32)


def solution(mesh):
    in_specs = (
        P("dp", "feat"),
        P("dp", "feat"),
        P("feat", None, None),
        P("feat", None, None),
        P("feat", None, None),
        P("feat", None, None),
        P("feat", None, None),
        P(),
        P(),
        P(),
    )
    out_specs = (P("feat", "dp", None), P("feat", "dp", None))
    return jax.shard_map(
        per_device, mesh=mesh, in_specs=in_specs, out_specs=out_specs, check_vma=False
    )
```

```python
import functools

import jax
import jax.numpy as jnp
from jax import lax
from jax.experimental import pallas as pl
from jax.experimental.pallas import tpu as pltpu
from jax.sharding import PartitionSpec as P

inv_root_two = 0.7071067811865476
inv_root_two_pi = 0.3989422804014327
STEP = 2
MESH = pl.DeviceIdType.MESH


def column_loop(columns, body):
    tile = min(columns, 256)

    @pl.loop(0, columns // tile)
    def _(step):
        body(pl.ds(pl.multiple_of(step * tile, tile), tile))


def gather_kernel(
    loaders,
    features,
    tok_ref,
    target_ref,
    send_sel_ref,
    take_sel_ref,
    fac_ref,
    tok_all,
    goal_all,
    fac_all,
    outgoing,
    arrived,
    slot_send,
    slot_recv,
    fac_send,
    fac_recv,
    chip_send,
    chip_recv,
    pair_send,
    pair_recv,
    line_send,
    line_recv,
):
    dev = lax.axis_index("dp")
    me = lax.axis_index("feat")
    columns = tok_ref.shape[1]
    slot = outgoing.shape[0] // loaders

    def to_dp(peer):
        return {"dp": peer}

    def to_feat(peer):
        return {"feat": peer}

    barrier = pltpu.get_barrier_semaphore()
    for off in range(1, loaders):
        pl.semaphore_signal(
            barrier, inc=1, device_id=to_dp(lax.rem(dev + off, loaders)), device_id_type=MESH
        )
    for off in range(1, features):
        pl.semaphore_signal(
            barrier, inc=1, device_id=to_feat(lax.rem(me + off, features)), device_id_type=MESH
        )
    pl.semaphore_wait(barrier, loaders + features - 2)

    def remote(src, dst, send, recv, target):
        return pltpu.make_async_remote_copy(
            src_ref=src,
            dst_ref=dst,
            send_sem=send,
            recv_sem=recv,
            device_id=target,
            device_id_type=MESH,
        )

    fac_copies = []
    for off in range(1, features):
        peer = lax.rem(me + off, features)
        fac_copies.append(
            remote(
                fac_ref.at[peer],
                fac_all.at[dev, me],
                fac_send.at[off - 1],
                fac_recv.at[off - 1],
                to_feat(peer),
            )
        )
        fac_copies[-1].start()
    fac_all[dev, me] = fac_ref[me]

    def hop(ref, which, step, right):
        shard = jnp.maximum(me - step, 0) if right else jnp.minimum(me + step, features - 1)
        peer = jnp.minimum(me + 1, features - 1) if right else jnp.maximum(me - 1, 0)
        side = 0 if right else 1
        return remote(
            ref.at[shard],
            ref.at[shard],
            line_send.at[which, side, step],
            line_recv.at[which, side, step],
            to_feat(peer),
        )

    def has(step, right):
        return (me >= step) if right else (me + step <= features - 1)

    def sends(step, right):
        return has(step, right) & ((me < features - 1) if right else (me > 0))

    def line_step(ref, which, step):
        for right in (True, False):
            if step > 0:

                @pl.when(has(step, right))
                def _():
                    hop(ref, which, step - 1, right).wait_recv()

            if step < features - 1:

                @pl.when(sends(step, right))
                def _():
                    hop(ref, which, step, right).start()

    def line_end(ref, which):
        for step in range(features - 1):
            for right in (True, False):

                @pl.when(sends(step, right))
                def _():
                    hop(ref, which, step, right).wait_send()

    def turn_tokens(cols):
        tok_all[me, cols, :] = tok_ref[:, cols].T

    column_loop(columns, turn_tokens)
    line_step(tok_all, 0, 0)

    def pick(cols):
        outgoing[:, cols] = jnp.dot(
            send_sel_ref[...], target_ref[:, cols], preferred_element_type=jnp.float32
        ).astype(jnp.bfloat16)

    column_loop(columns, pick)
    slot_copies = []
    for off in range(1, loaders):
        peer = lax.rem(dev + off, loaders)
        slot_copies.append(
            remote(
                outgoing.at[pl.ds(pl.multiple_of(peer * slot, slot), slot)],
                arrived.at[pl.ds(pl.multiple_of(dev * slot, slot), slot)],
                slot_send.at[off - 1],
                slot_recv.at[off - 1],
                to_dp(peer),
            )
        )
        slot_copies[-1].start()
    own = pl.ds(pl.multiple_of(dev * slot, slot), slot)
    arrived[own] = outgoing[own]

    for copy in fac_copies:
        copy.wait_recv()
    chips = loaders // 2
    chip = dev // 2
    core = lax.rem(dev, 2)
    sibling = dev + 1 - 2 * core

    def to_pair(index, piece):
        return remote(
            fac_all.at[piece],
            fac_all.at[piece],
            pair_send.at[index],
            pair_recv.at[index],
            to_dp(sibling),
        )

    pair_copies = [to_pair(0, dev)]
    pair_copies[0].start()
    chip_copies = []
    for off in range(1, chips):
        peer = lax.rem(chip + off, chips) * 2 + core
        chip_copies.append(
            remote(
                fac_all.at[dev],
                fac_all.at[dev],
                chip_send.at[off - 1],
                chip_recv.at[off - 1],
                to_dp(peer),
            )
        )
        chip_copies[-1].start()

    if features > 2:
        line_step(tok_all, 0, 1)
    for copy in slot_copies:
        copy.wait_recv()

    def take(cols):
        goal_all[me, cols, :] = lax.dot_general(
            arrived[:, cols],
            take_sel_ref[...],
            (((0,), (0,)), ((), ())),
            preferred_element_type=jnp.float32,
        ).astype(jnp.bfloat16)

    column_loop(columns, take)
    line_step(goal_all, 1, 0)
    for step in range(2, features):
        line_step(tok_all, 0, step)
    for off in range(1, chips):
        chip_copies[off - 1].wait_recv()
        piece = lax.rem(chip + chips - off, chips) * 2 + core
        pair_copies.append(to_pair(off, piece))
        pair_copies[-1].start()
    for step in range(1, features):
        line_step(goal_all, 1, step)
    for copy in pair_copies:
        copy.wait()
    for copy in slot_copies + fac_copies + chip_copies:
        copy.wait_send()
    line_end(tok_all, 0)
    line_end(goal_all, 1)


def gather_stage(loaders, features, tokens, targets, send_sel, take_sel, factors):
    rows, columns = tokens.shape
    slots = send_sel.shape[0]
    dma = pltpu.SemaphoreType.DMA
    vmem = pl.BlockSpec(memory_space=pltpu.VMEM)
    return pl.pallas_call(
        functools.partial(gather_kernel, loaders, features),
        in_specs=[vmem] * 5,
        out_specs=[vmem] * 3,
        out_shape=[
            jax.ShapeDtypeStruct((features, columns, rows), jnp.bfloat16),
            jax.ShapeDtypeStruct((features, columns, rows), jnp.bfloat16),
            jax.ShapeDtypeStruct((loaders,) + factors.shape, jnp.bfloat16),
        ],
        scratch_shapes=[
            pltpu.VMEM((slots, columns), jnp.bfloat16),
            pltpu.VMEM((slots, columns), jnp.bfloat16),
            dma((loaders - 1,)),
            dma((loaders - 1,)),
            dma((features - 1,)),
            dma((features - 1,)),
            dma((loaders // 2 - 1,)),
            dma((loaders // 2 - 1,)),
            dma((loaders // 2,)),
            dma((loaders // 2,)),
            dma((2, 2, features - 1)),
            dma((2, 2, features - 1)),
        ],
        compiler_params=pltpu.CompilerParams(
            collective_id=0, has_side_effects=True, vmem_limit_bytes=48 * 1024 * 1024
        ),
    )(tokens, targets, send_sel, take_sel, factors)


def reduce_kernel(
    loaders,
    features,
    mix_ref,
    fir_ref,
    mix_out,
    fir_out,
    mix_pair,
    fir_pair,
    mix_sum,
    fir_sum,
    mix_got,
    fir_got,
    fir_total,
    pair_send,
    pair_recv,
    chip_send,
    chip_recv,
    feat_send,
    feat_recv,
):
    dev = lax.axis_index("dp")
    me = lax.axis_index("feat")
    chips = loaders // 2
    chip = dev // 2
    core = lax.rem(dev, 2)
    sibling = dev + 1 - 2 * core

    def chip_at(off):
        return lax.rem(chip + off, chips)

    targets = [{"dp": sibling}]
    targets += [{"dp": chip_at(off) * 2 + core} for off in range(1, chips)]
    targets += [{"feat": lax.rem(me + off, features)} for off in range(1, features)]
    barrier = pltpu.get_barrier_semaphore()
    for target in targets:
        pl.semaphore_signal(barrier, inc=1, device_id=target, device_id_type=MESH)
    pl.semaphore_wait(barrier, len(targets))

    def remote(src, dst, send, recv, target):
        return pltpu.make_async_remote_copy(
            src_ref=src,
            dst_ref=dst,
            send_sem=send,
            recv_sem=recv,
            device_id=target,
            device_id_type=MESH,
        )

    parts = ((fir_ref, fir_pair, fir_sum, fir_got), (mix_ref, mix_pair, mix_sum, mix_got))
    order = list(range(1, chips)) + [0]
    pairs = {}
    for which, (ref, pair, _, _) in enumerate(parts):
        for off in order:
            there = chip_at(off)
            pairs[which, off] = remote(
                ref.at[there * 2 + 1 - core],
                pair.at[there],
                pair_send.at[which, off],
                pair_recv.at[which, off],
                {"dp": sibling},
            )
            pairs[which, off].start()

    def each(count, body):
        @pl.loop(0, count)
        def _(index):
            body(index)

    sent = {}
    for which, (ref, pair, total, got) in enumerate(parts):
        for off in range(1, chips):
            there = chip_at(off)
            pairs[which, off].wait_recv()

            def add(index):
                total[there, index] = (
                    ref[there * 2 + core, index].astype(jnp.float32)
                    + pair[there, index].astype(jnp.float32)
                ).astype(jnp.bfloat16)

            each(ref.shape[1], add)
            sent[which, off] = remote(
                total.at[there],
                got.at[off - 1],
                chip_send.at[which, off - 1],
                chip_recv.at[which, off - 1],
                {"dp": there * 2 + core},
            )
            sent[which, off].start()

    def finish(which, store):
        ref, pair, _, got = parts[which]
        pairs[which, 0].wait_recv()
        for off in range(1, chips):
            sent[which, off].wait_recv()

        def add(index):
            value = ref[dev, index].astype(jnp.float32) + pair[chip, index].astype(jnp.float32)
            for off in range(1, chips):
                value = value + got[off - 1, index].astype(jnp.float32)
            store(index, value)

        each(ref.shape[1], add)

    def store_first(index, value):
        fir_total[index] = value.astype(jnp.bfloat16)

    def store_mixed(index, value):
        mix_out[index] = value

    finish(0, store_first)
    last = []
    for off in range(1, features):
        peer = lax.rem(me + off, features)
        last.append(
            remote(
                fir_total.at[peer],
                fir_out.at[me],
                feat_send.at[off - 1],
                feat_recv.at[off - 1],
                {"feat": peer},
            )
        )
        last[-1].start()
    fir_out[me] = fir_total[me]
    finish(1, store_mixed)
    for copy in last:
        copy.wait()
    for copy in list(pairs.values()) + list(sent.values()):
        copy.wait_send()


def reduce_stage(loaders, features, mixed, first):
    chips = loaders // 2
    dma = pltpu.SemaphoreType.DMA
    vmem = pl.BlockSpec(memory_space=pltpu.VMEM)

    def buffers(count):
        return [pltpu.VMEM((count,) + a.shape[1:], jnp.bfloat16) for a in (mixed, first)]

    return pl.pallas_call(
        functools.partial(reduce_kernel, loaders, features),
        in_specs=[vmem] * 2,
        out_specs=[vmem] * 2,
        out_shape=[
            jax.ShapeDtypeStruct(mixed.shape[1:], jnp.float32),
            jax.ShapeDtypeStruct(first.shape[1:], jnp.bfloat16),
        ],
        scratch_shapes=buffers(chips)
        + buffers(chips)
        + buffers(chips - 1)
        + [
            pltpu.VMEM(first.shape[1:], jnp.bfloat16),
            dma((2, chips)),
            dma((2, chips)),
            dma((2, chips - 1)),
            dma((2, chips - 1)),
            dma((features - 1,)),
            dma((features - 1,)),
        ],
        compiler_params=pltpu.CompilerParams(
            collective_id=1, has_side_effects=True, vmem_limit_bytes=48 * 1024 * 1024
        ),
    )(mixed, first)


def mixed_kernel(act_ref, tan_ref, grad_ref, fac_ref, fac_tan_ref, hess_ref, back_ref):
    rows = act_ref.shape[2]
    for b in range(act_ref.shape[0]):
        act = act_ref[b]
        tan = tan_ref[b]
        fac = fac_ref[b]
        fac_tan = fac_tan_ref[b]
        first_dims = (((0,), (0,)), ((), ()))
        both = lax.dot_general(
            fac,
            jnp.concatenate([act, tan], axis=1),
            first_dims,
            preferred_element_type=jnp.float32,
        )
        pre_act = both[:, :rows]
        pre_tan = both[:, rows:] + lax.dot_general(
            fac_tan, act, first_dims, preferred_element_type=jnp.float32
        )
        grad = grad_ref[b].astype(jnp.float32)
        density = jnp.exp(-0.5 * pre_act * pre_act) * inv_root_two_pi
        cdf = 0.5 * (1.0 + lax.erf(pre_act * inv_root_two))
        pre_grad = (grad * (cdf + pre_act * density)).astype(jnp.bfloat16)
        pre_tan_grad = (grad * (density * (2.0 - pre_act * pre_act)) * pre_tan).astype(
            jnp.bfloat16
        )
        hess = lax.dot_general(
            jnp.concatenate([tan, act], axis=1),
            jnp.concatenate([pre_grad, pre_tan_grad], axis=1),
            (((1,), (1,)), ((), ())),
            preferred_element_type=jnp.float32,
        )
        parts, _, share, width = hess_ref.shape
        hess_ref[:, b] = hess.reshape(parts, share, width).astype(hess_ref.dtype)
        back_ref[b] = (
            jnp.dot(fac, pre_tan_grad, preferred_element_type=jnp.float32)
            + jnp.dot(fac_tan, pre_grad, preferred_element_type=jnp.float32)
        ).astype(back_ref.dtype)


def mixed_stage(loaders, act, tan, grad, fac, fac_tan):
    blocks, width, rows = act.shape
    thin = pl.BlockSpec((STEP, width, rows), lambda s: (s, 0, 0))
    wide = pl.BlockSpec((STEP, width, width), lambda s: (s, 0, 0))
    share = width // loaders
    split = pl.BlockSpec((loaders, STEP, share, width), lambda s: (0, s, 0, 0))
    return pl.pallas_call(
        mixed_kernel,
        grid=(blocks // STEP,),
        in_specs=[thin, thin, thin, wide, wide],
        out_specs=[split, thin],
        out_shape=[
            jax.ShapeDtypeStruct((loaders, blocks, share, width), jnp.bfloat16),
            jax.ShapeDtypeStruct((blocks, width, rows), jnp.bfloat16),
        ],
        compiler_params=pltpu.CompilerParams(vmem_limit_bytes=32 * 1024 * 1024),
        cost_estimate=pl.CostEstimate(
            flops=14 * blocks * width * width * rows,
            bytes_accessed=blocks * width * (6 * width + 8 * rows),
            transcendentals=2 * blocks * width * rows,
        ),
    )(act, tan, grad, fac, fac_tan)


def per_device(
    tokens,
    targets,
    first_blocks,
    second_factor_blocks,
    down_blocks,
    first_tangent,
    second_factor_tangent,
    doc_lengths,
    doc_owners,
    pack_offsets,
):
    loaders = lax.axis_size("dp")
    features = lax.axis_size("feat")
    device = lax.axis_index("dp")
    tok_count, feature_cols = tokens.shape
    pack_rows = targets.shape[0]
    slot_rows = -(-2 * tok_count // (16 * loaders)) * 16
    local_blocks, block_in, block_out = first_blocks.shape
    all_blocks = local_blocks * features
    local_out = block_out // features
    pair = local_out // local_blocks

    position = jnp.arange(slot_rows, dtype=jnp.int32)
    mine = (doc_owners == device).astype(jnp.int32)
    slot_start = jnp.sum(mine * pack_offsets, axis=1)
    pack_source = (slot_start[:, None] + position[None, :]).reshape(-1)
    send_sel = (
        pack_source[:, None] == jnp.arange(pack_rows, dtype=jnp.int32)[None, :]
    ).astype(jnp.bfloat16)
    my_lengths = lax.dynamic_index_in_dim(doc_lengths, device, 0, keepdims=False)
    my_owners = lax.dynamic_index_in_dim(doc_owners, device, 0, keepdims=False)
    my_starts = jnp.cumsum(my_lengths) - my_lengths
    row = jnp.arange(tok_count, dtype=jnp.int32)
    inside = (row[:, None] >= my_starts[None, :]) & (
        row[:, None] < (my_starts + my_lengths)[None, :]
    )
    inside_int = inside.astype(jnp.int32)
    source = jnp.sum(inside_int * (my_owners * slot_rows - my_starts)[None, :], axis=1) + row
    weight = jnp.sum(inside.astype(jnp.float32) / my_lengths.astype(jnp.float32)[None, :], axis=1)
    take_sel = (
        jnp.arange(loaders * slot_rows, dtype=jnp.int32)[:, None] == source[None, :]
    ).astype(jnp.bfloat16)

    rows = local_blocks * block_in
    share = rows // loaders
    factors = jnp.stack(
        [
            lax.dynamic_slice_in_dim(w.reshape(rows, block_out), device * share, share, 0)
            for w in (first_blocks, first_tangent, jnp.swapaxes(down_blocks, 1, 2))
        ]
    )
    factors = factors.reshape(3, share, features, local_out).transpose(2, 0, 3, 1)
    factors = factors.reshape(features, 3 * local_out, share)
    tok_all, goal_all, factors = gather_stage(
        loaders, features, tokens, targets, send_sel, take_sel, factors
    )
    factors = factors.reshape(loaders, features, 3, local_out, share)
    factors = factors.transpose(2, 3, 1, 0, 4).reshape(3, local_out, all_blocks, block_in)
    tok_all = tok_all.reshape(all_blocks, block_in, tok_count)
    goal_all = goal_all.reshape(all_blocks, block_in, tok_count)

    def mix(values):
        return (
            values.astype(jnp.bfloat16)
            .reshape(all_blocks, local_blocks, pair, tok_count)
            .transpose(1, 0, 2, 3)
            .reshape(local_blocks, block_out, tok_count)
        )

    def first(weights, rows_of):
        return jnp.einsum("jki,kir->kjr", weights, rows_of, preferred_element_type=jnp.float32)

    act = mix(first(factors[0], tok_all))
    tan = mix(first(factors[1], tok_all))
    grad = mix(first(factors[2], goal_all) * weight)
    hess_mixed, back = mixed_stage(
        loaders, act, tan, grad, second_factor_blocks, second_factor_tangent
    )

    back = (
        back.reshape(local_blocks, all_blocks, pair, tok_count)
        .transpose(1, 0, 2, 3)
        .reshape(all_blocks, local_out, tok_count)
    )
    hess_first = jnp.einsum("kjr,kir->kij", back, tok_all, preferred_element_type=jnp.float32)
    in_share = block_in // loaders
    hess_first = hess_first.astype(jnp.bfloat16).reshape(
        all_blocks, loaders, in_share * local_out
    )
    hess_first = hess_first.transpose(1, 0, 2).reshape(
        loaders, features, local_blocks, in_share * local_out
    )
    hess_mixed, hess_first = reduce_stage(loaders, features, hess_mixed, hess_first)
    hess_first = (
        hess_first.reshape(features, local_blocks, in_share, local_out)
        .transpose(1, 2, 0, 3)
        .reshape(local_blocks, in_share, block_out)
    )
    return hess_first.astype(jnp.float32), hess_mixed


def solution(mesh):
    in_specs = (
        P("dp", "feat"),
        P("dp", "feat"),
        P("feat", None, None),
        P("feat", None, None),
        P("feat", None, None),
        P("feat", None, None),
        P("feat", None, None),
        P(),
        P(),
        P(),
    )
    out_specs = (P("feat", "dp", None), P("feat", "dp", None))
    return jax.shard_map(
        per_device, mesh=mesh, in_specs=in_specs, out_specs=out_specs, check_vma=False
    )
```

```python
import functools

import jax
import jax.numpy as jnp
import numpy as np
from jax import lax
from jax.experimental import pallas as pl
from jax.experimental.pallas import tpu as pltpu
from jax.sharding import PartitionSpec as P

inv_root_two = 0.7071067811865476
inv_root_two_pi = 0.3989422804014327
STEP = 2
MESH = pl.DeviceIdType.MESH


def column_loop(columns, body):
    tile = min(columns, 256)

    @pl.loop(0, columns // tile)
    def _(step):
        body(pl.ds(pl.multiple_of(step * tile, tile), tile))


def gather_kernel(loaders, features, fused, *refs):
    if fused:
        spread_ref, keep_ref, weight_ref = refs[5:8]
        act_out, tan_out, grad_out = refs[9:12]
        refs = refs[:5] + (refs[8],) + refs[12:]
    tok_ref, target_ref, send_sel_ref, take_sel_ref, fac_ref = refs[:5]
    tok_all, goal_all, fac_all, outgoing, arrived = refs[5:10]
    slot_send, slot_recv, fac_send, fac_recv, chip_send, chip_recv = refs[10:16]
    pair_send, pair_recv, line_send, line_recv = refs[16:]
    dev = lax.axis_index("dp")
    me = lax.axis_index("feat")
    columns = tok_ref.shape[1]
    slot = outgoing.shape[0] // loaders

    def to_dp(peer):
        return {"dp": peer}

    def to_feat(peer):
        return {"feat": peer}

    barrier = pltpu.get_barrier_semaphore()
    for off in range(1, loaders):
        pl.semaphore_signal(
            barrier, inc=1, device_id=to_dp(lax.rem(dev + off, loaders)), device_id_type=MESH
        )
    for off in range(1, features):
        pl.semaphore_signal(
            barrier, inc=1, device_id=to_feat(lax.rem(me + off, features)), device_id_type=MESH
        )
    pl.semaphore_wait(barrier, loaders + features - 2)

    def remote(src, dst, send, recv, target):
        return pltpu.make_async_remote_copy(
            src_ref=src,
            dst_ref=dst,
            send_sem=send,
            recv_sem=recv,
            device_id=target,
            device_id_type=MESH,
        )

    fac_copies = []
    for off in range(1, features):
        peer = lax.rem(me + off, features)
        fac_copies.append(
            remote(
                fac_ref.at[peer],
                fac_all.at[dev, me],
                fac_send.at[off - 1],
                fac_recv.at[off - 1],
                to_feat(peer),
            )
        )
        fac_copies[-1].start()
    fac_all[dev, me] = fac_ref[me]

    def hop(ref, which, step, right):
        shard = jnp.maximum(me - step, 0) if right else jnp.minimum(me + step, features - 1)
        peer = jnp.minimum(me + 1, features - 1) if right else jnp.maximum(me - 1, 0)
        side = 0 if right else 1
        return remote(
            ref.at[shard],
            ref.at[shard],
            line_send.at[which, side, step],
            line_recv.at[which, side, step],
            to_feat(peer),
        )

    def has(step, right):
        return (me >= step) if right else (me + step <= features - 1)

    def sends(step, right):
        return has(step, right) & ((me < features - 1) if right else (me > 0))

    def line_step(ref, which, step):
        for right in (True, False):
            if step > 0:

                @pl.when(has(step, right))
                def _():
                    hop(ref, which, step - 1, right).wait_recv()

            if step < features - 1:

                @pl.when(sends(step, right))
                def _():
                    hop(ref, which, step, right).start()

    def line_end(ref, which):
        for step in range(features - 1):
            for right in (True, False):

                @pl.when(sends(step, right))
                def _():
                    hop(ref, which, step, right).wait_send()

    def turn_tokens(cols):
        tok_all[me, cols, :] = tok_ref[:, cols].T

    column_loop(columns, turn_tokens)
    line_step(tok_all, 0, 0)

    def pick(cols):
        outgoing[:, cols] = jnp.dot(
            send_sel_ref[...], target_ref[:, cols], preferred_element_type=jnp.float32
        ).astype(jnp.bfloat16)

    column_loop(columns, pick)
    slot_copies = []
    for off in range(1, loaders):
        peer = lax.rem(dev + off, loaders)
        slot_copies.append(
            remote(
                outgoing.at[pl.ds(pl.multiple_of(peer * slot, slot), slot)],
                arrived.at[pl.ds(pl.multiple_of(dev * slot, slot), slot)],
                slot_send.at[off - 1],
                slot_recv.at[off - 1],
                to_dp(peer),
            )
        )
        slot_copies[-1].start()
    own = pl.ds(pl.multiple_of(dev * slot, slot), slot)
    arrived[own] = outgoing[own]

    for copy in fac_copies:
        copy.wait_recv()
    chips = loaders // 2
    chip = dev // 2
    core = lax.rem(dev, 2)
    sibling = dev + 1 - 2 * core

    def to_pair(index, piece):
        return remote(
            fac_all.at[piece],
            fac_all.at[piece],
            pair_send.at[index],
            pair_recv.at[index],
            to_dp(sibling),
        )

    pair_copies = [to_pair(0, dev)]
    pair_copies[0].start()
    chip_copies = []
    for off in range(1, chips):
        peer = lax.rem(chip + off, chips) * 2 + core
        chip_copies.append(
            remote(
                fac_all.at[dev],
                fac_all.at[dev],
                chip_send.at[off - 1],
                chip_recv.at[off - 1],
                to_dp(peer),
            )
        )
        chip_copies[-1].start()

    if features > 2:
        line_step(tok_all, 0, 1)
    for copy in slot_copies:
        copy.wait_recv()

    def take(cols):
        goal_all[me, cols, :] = lax.dot_general(
            arrived[:, cols],
            take_sel_ref[...],
            (((0,), (0,)), ((), ())),
            preferred_element_type=jnp.float32,
        ).astype(jnp.bfloat16)

    column_loop(columns, take)
    line_step(goal_all, 1, 0)
    for step in range(2, features - 1):
        line_step(tok_all, 0, step)
    for off in range(1, chips):
        chip_copies[off - 1].wait_recv()
        piece = lax.rem(chip + chips - off, chips) * 2 + core
        pair_copies.append(to_pair(off, piece))
        pair_copies[-1].start()
    line_step(goal_all, 1, 1)
    line_step(tok_all, 0, features - 1)
    for copy in pair_copies:
        copy.wait()

    def first_stage(src, uses, lo, hi, near, far):
        if not fused:
            return
        per_shard, pieces = fused
        tall, wide = keep_ref.shape
        width = tall // act_out.shape[0]
        out_rows = spread_ref.shape[1]

        @pl.loop(lo * per_shard, hi * per_shard)
        def _(unit):
            shard = unit // per_shard
            part = unit % per_shard
            distance = jnp.maximum(shard - me, me - shard)

            @pl.when((distance >= near) & (distance <= far))
            def _():
                cols = src[shard, pl.ds(pl.multiple_of(part * wide, wide), wide), :]
                for which, out in uses:
                    rows = slice(which * out_rows, (which + 1) * out_rows)
                    compact = jnp.concatenate(
                        [fac_all[part * pieces + n, shard, rows, :] for n in range(pieces)], axis=1
                    )
                    spread = jnp.dot(
                        spread_ref[...], compact, preferred_element_type=jnp.float32
                    ).astype(jnp.bfloat16)
                    value = jnp.dot(
                        spread * keep_ref[...], cols, preferred_element_type=jnp.float32
                    )
                    if which == 2:
                        value = value * weight_ref[...]
                    place = pl.ds(pl.multiple_of(unit * width, width), width)
                    out[:, place, :] = value.reshape(out.shape[0], width, out.shape[2]).astype(
                        out.dtype
                    )

    if fused:
        on_tok = ((0, act_out), (1, tan_out))
        on_goal = ((2, grad_out),)
    else:
        on_tok = on_goal = ()
    half = features // 2
    first_stage(tok_all, on_tok, 0, half, 0, features)
    for step in range(2, features - 1):
        line_step(goal_all, 1, step)
    first_stage(tok_all, on_tok, half, features, 0, features)
    first_stage(goal_all, on_goal, 0, features, 0, features - 2)
    line_step(goal_all, 1, features - 1)
    first_stage(goal_all, on_goal, 0, features, features - 1, features)
    for copy in slot_copies + fac_copies + chip_copies:
        copy.wait_send()
    line_end(tok_all, 0)
    line_end(goal_all, 1)


def gather_stage(loaders, features, operands, fused):
    tokens, _, send_sel, _, factors = operands[:5]
    rows, columns = tokens.shape
    slots = send_sel.shape[0]
    dma = pltpu.SemaphoreType.DMA
    vmem = pl.BlockSpec(memory_space=pltpu.VMEM)
    shards = jax.ShapeDtypeStruct((features, columns, rows), jnp.bfloat16)
    pieces = jax.ShapeDtypeStruct((loaders,) + factors.shape, jnp.bfloat16)
    out_shape = [shards, shards, pieces]
    held = []
    if fused:
        local_out = factors.shape[1] // 3
        blocks = operands[5].shape[0] // 16
        mixed = jax.ShapeDtypeStruct((blocks, features * local_out, rows), jnp.bfloat16)
        held = [pltpu.VMEM(a.shape, a.dtype) for a in out_shape[1:]]
        out_shape = [shards, mixed, mixed, mixed]
    return pl.pallas_call(
        functools.partial(gather_kernel, loaders, features, fused),
        in_specs=[vmem] * len(operands),
        out_specs=[vmem] * len(out_shape),
        out_shape=out_shape,
        scratch_shapes=held
        + [
            pltpu.VMEM((slots, columns), jnp.bfloat16),
            pltpu.VMEM((slots, columns), jnp.bfloat16),
            dma((loaders - 1,)),
            dma((loaders - 1,)),
            dma((features - 1,)),
            dma((features - 1,)),
            dma((loaders // 2 - 1,)),
            dma((loaders // 2 - 1,)),
            dma((loaders // 2,)),
            dma((loaders // 2,)),
            dma((2, 2, features - 1)),
            dma((2, 2, features - 1)),
        ],
        compiler_params=pltpu.CompilerParams(
            collective_id=0, has_side_effects=True, vmem_limit_bytes=48 * 1024 * 1024
        ),
    )(*operands)


def reduce_kernel(
    loaders,
    features,
    mix_ref,
    fir_ref,
    mix_out,
    fir_out,
    mix_pair,
    fir_pair,
    mix_sum,
    fir_sum,
    mix_got,
    fir_got,
    fir_total,
    pair_send,
    pair_recv,
    chip_send,
    chip_recv,
    feat_send,
    feat_recv,
):
    dev = lax.axis_index("dp")
    me = lax.axis_index("feat")
    chips = loaders // 2
    chip = dev // 2
    core = lax.rem(dev, 2)
    sibling = dev + 1 - 2 * core

    def chip_at(off):
        return lax.rem(chip + off, chips)

    targets = [{"dp": sibling}]
    targets += [{"dp": chip_at(off) * 2 + core} for off in range(1, chips)]
    targets += [{"feat": lax.rem(me + off, features)} for off in range(1, features)]
    barrier = pltpu.get_barrier_semaphore()
    for target in targets:
        pl.semaphore_signal(barrier, inc=1, device_id=target, device_id_type=MESH)
    pl.semaphore_wait(barrier, len(targets))

    def remote(src, dst, send, recv, target):
        return pltpu.make_async_remote_copy(
            src_ref=src,
            dst_ref=dst,
            send_sem=send,
            recv_sem=recv,
            device_id=target,
            device_id_type=MESH,
        )

    parts = ((fir_ref, fir_pair, fir_sum, fir_got), (mix_ref, mix_pair, mix_sum, mix_got))
    order = list(range(1, chips)) + [0]
    pairs = {}
    for which, (ref, pair, _, _) in enumerate(parts):
        for off in order:
            there = chip_at(off)
            pairs[which, off] = remote(
                ref.at[there * 2 + 1 - core],
                pair.at[there],
                pair_send.at[which, off],
                pair_recv.at[which, off],
                {"dp": sibling},
            )
            pairs[which, off].start()

    def each(count, body):
        @pl.loop(0, count)
        def _(index):
            body(index)

    sent = {}
    for which, (ref, pair, total, got) in enumerate(parts):
        for off in range(1, chips):
            there = chip_at(off)
            pairs[which, off].wait_recv()

            def add(index):
                total[there, index] = (
                    ref[there * 2 + core, index].astype(jnp.float32)
                    + pair[there, index].astype(jnp.float32)
                ).astype(jnp.bfloat16)

            each(ref.shape[1], add)
            sent[which, off] = remote(
                total.at[there],
                got.at[off - 1],
                chip_send.at[which, off - 1],
                chip_recv.at[which, off - 1],
                {"dp": there * 2 + core},
            )
            sent[which, off].start()

    def finish(which, store):
        ref, pair, _, got = parts[which]
        pairs[which, 0].wait_recv()
        for off in range(1, chips):
            sent[which, off].wait_recv()

        def add(index):
            value = ref[dev, index].astype(jnp.float32) + pair[chip, index].astype(jnp.float32)
            for off in range(1, chips):
                value = value + got[off - 1, index].astype(jnp.float32)
            store(index, value)

        each(ref.shape[1], add)

    def store_first(index, value):
        fir_total[index] = value.astype(jnp.bfloat16)

    def store_mixed(index, value):
        mix_out[index] = value

    finish(0, store_first)
    last = []
    for off in range(1, features):
        peer = lax.rem(me + off, features)
        last.append(
            remote(
                fir_total.at[peer],
                fir_out.at[me],
                feat_send.at[off - 1],
                feat_recv.at[off - 1],
                {"feat": peer},
            )
        )
        last[-1].start()
    fir_out[me] = fir_total[me]
    finish(1, store_mixed)
    for copy in last:
        copy.wait()
    for copy in list(pairs.values()) + list(sent.values()):
        copy.wait_send()


def reduce_stage(loaders, features, mixed, first):
    chips = loaders // 2
    dma = pltpu.SemaphoreType.DMA
    vmem = pl.BlockSpec(memory_space=pltpu.VMEM)

    def buffers(count):
        return [pltpu.VMEM((count,) + a.shape[1:], jnp.bfloat16) for a in (mixed, first)]

    return pl.pallas_call(
        functools.partial(reduce_kernel, loaders, features),
        in_specs=[vmem] * 2,
        out_specs=[vmem] * 2,
        out_shape=[
            jax.ShapeDtypeStruct(mixed.shape[1:], jnp.float32),
            jax.ShapeDtypeStruct(first.shape[1:], jnp.bfloat16),
        ],
        scratch_shapes=buffers(chips)
        + buffers(chips)
        + buffers(chips - 1)
        + [
            pltpu.VMEM(first.shape[1:], jnp.bfloat16),
            dma((2, chips)),
            dma((2, chips)),
            dma((2, chips - 1)),
            dma((2, chips - 1)),
            dma((features - 1,)),
            dma((features - 1,)),
        ],
        compiler_params=pltpu.CompilerParams(
            collective_id=1, has_side_effects=True, vmem_limit_bytes=48 * 1024 * 1024
        ),
    )(mixed, first)


def mixed_kernel(act_ref, tan_ref, grad_ref, fac_ref, fac_tan_ref, hess_ref, back_ref):
    rows = act_ref.shape[2]
    for b in range(act_ref.shape[0]):
        act = act_ref[b]
        tan = tan_ref[b]
        fac = fac_ref[b]
        fac_tan = fac_tan_ref[b]
        first_dims = (((0,), (0,)), ((), ()))
        both = lax.dot_general(
            fac,
            jnp.concatenate([act, tan], axis=1),
            first_dims,
            preferred_element_type=jnp.float32,
        )
        pre_act = both[:, :rows]
        pre_tan = both[:, rows:] + lax.dot_general(
            fac_tan, act, first_dims, preferred_element_type=jnp.float32
        )
        grad = grad_ref[b].astype(jnp.float32)
        density = jnp.exp(-0.5 * pre_act * pre_act) * inv_root_two_pi
        cdf = 0.5 * (1.0 + lax.erf(pre_act * inv_root_two))
        pre_grad = (grad * (cdf + pre_act * density)).astype(jnp.bfloat16)
        pre_tan_grad = (grad * (density * (2.0 - pre_act * pre_act)) * pre_tan).astype(
            jnp.bfloat16
        )
        hess = lax.dot_general(
            jnp.concatenate([tan, act], axis=1),
            jnp.concatenate([pre_grad, pre_tan_grad], axis=1),
            (((1,), (1,)), ((), ())),
            preferred_element_type=jnp.float32,
        )
        parts, _, share, width = hess_ref.shape
        hess_ref[:, b] = hess.reshape(parts, share, width).astype(hess_ref.dtype)
        back_ref[b] = (
            jnp.dot(fac, pre_tan_grad, preferred_element_type=jnp.float32)
            + jnp.dot(fac_tan, pre_grad, preferred_element_type=jnp.float32)
        ).astype(back_ref.dtype)


def mixed_stage(loaders, act, tan, grad, fac, fac_tan):
    blocks, width, rows = act.shape
    thin = pl.BlockSpec((STEP, width, rows), lambda s: (s, 0, 0))
    wide = pl.BlockSpec((STEP, width, width), lambda s: (s, 0, 0))
    share = width // loaders
    split = pl.BlockSpec((loaders, STEP, share, width), lambda s: (0, s, 0, 0))
    return pl.pallas_call(
        mixed_kernel,
        grid=(blocks // STEP,),
        in_specs=[thin, thin, thin, wide, wide],
        out_specs=[split, thin],
        out_shape=[
            jax.ShapeDtypeStruct((loaders, blocks, share, width), jnp.bfloat16),
            jax.ShapeDtypeStruct((blocks, width, rows), jnp.bfloat16),
        ],
        compiler_params=pltpu.CompilerParams(vmem_limit_bytes=32 * 1024 * 1024),
        cost_estimate=pl.CostEstimate(
            flops=14 * blocks * width * width * rows,
            bytes_accessed=blocks * width * (6 * width + 8 * rows),
            transcendentals=2 * blocks * width * rows,
        ),
    )(act, tan, grad, fac, fac_tan)


def per_device(
    tokens,
    targets,
    first_blocks,
    second_factor_blocks,
    down_blocks,
    first_tangent,
    second_factor_tangent,
    doc_lengths,
    doc_owners,
    pack_offsets,
):
    loaders = lax.axis_size("dp")
    features = lax.axis_size("feat")
    device = lax.axis_index("dp")
    tok_count, feature_cols = tokens.shape
    pack_rows = targets.shape[0]
    slot_rows = -(-2 * tok_count // (16 * loaders)) * 16
    local_blocks, block_in, block_out = first_blocks.shape
    all_blocks = local_blocks * features
    local_out = block_out // features
    pair = local_out // local_blocks

    position = jnp.arange(slot_rows, dtype=jnp.int32)
    mine = (doc_owners == device).astype(jnp.int32)
    slot_start = jnp.sum(mine * pack_offsets, axis=1)
    pack_source = (slot_start[:, None] + position[None, :]).reshape(-1)
    send_sel = (
        pack_source[:, None] == jnp.arange(pack_rows, dtype=jnp.int32)[None, :]
    ).astype(jnp.bfloat16)
    my_lengths = lax.dynamic_index_in_dim(doc_lengths, device, 0, keepdims=False)
    my_owners = lax.dynamic_index_in_dim(doc_owners, device, 0, keepdims=False)
    my_starts = jnp.cumsum(my_lengths) - my_lengths
    row = jnp.arange(tok_count, dtype=jnp.int32)
    inside = (row[:, None] >= my_starts[None, :]) & (
        row[:, None] < (my_starts + my_lengths)[None, :]
    )
    inside_int = inside.astype(jnp.int32)
    source = jnp.sum(inside_int * (my_owners * slot_rows - my_starts)[None, :], axis=1) + row
    weight = jnp.sum(inside.astype(jnp.float32) / my_lengths.astype(jnp.float32)[None, :], axis=1)
    take_sel = (
        jnp.arange(loaders * slot_rows, dtype=jnp.int32)[:, None] == source[None, :]
    ).astype(jnp.bfloat16)

    rows = local_blocks * block_in
    share = rows // loaders
    factors = jnp.stack(
        [
            lax.dynamic_slice_in_dim(w.reshape(rows, block_out), device * share, share, 0)
            for w in (first_blocks, first_tangent, jnp.swapaxes(down_blocks, 1, 2))
        ]
    )
    factors = factors.reshape(3, share, features, local_out).transpose(2, 0, 3, 1)
    factors = factors.reshape(features, 3 * local_out, share)
    group = 16 // pair
    wide = group * block_in
    whole_pieces = share % block_in == 0 and wide % share == 0 and local_blocks % group == 0
    fused = (local_blocks // group, wide // share) if whole_pieces else None
    operands = (tokens, targets, send_sel, take_sel, factors)
    if fused:
        out_row = np.arange(16 * local_blocks)
        column = (out_row // 16) * pair + out_row % pair
        spread = column[:, None] == np.arange(local_out)[None, :]
        keep = ((out_row % 16) // pair)[:, None] == (np.arange(wide) // block_in)[None, :]
        operands += (
            jnp.asarray(spread, jnp.bfloat16),
            jnp.asarray(keep, jnp.bfloat16),
            weight[None, :],
        )
        tok_all, act, tan, grad = gather_stage(loaders, features, operands, fused)
        tok_all = tok_all.reshape(all_blocks, block_in, tok_count)
    else:
        tok_all, goal_all, factors = gather_stage(loaders, features, operands, None)
        factors = factors.reshape(loaders, features, 3, local_out, share)
        factors = factors.transpose(2, 3, 1, 0, 4).reshape(3, local_out, all_blocks, block_in)
        tok_all = tok_all.reshape(all_blocks, block_in, tok_count)
        goal_all = goal_all.reshape(all_blocks, block_in, tok_count)

        def mix(values):
            return (
                values.astype(jnp.bfloat16)
                .reshape(all_blocks, local_blocks, pair, tok_count)
                .transpose(1, 0, 2, 3)
                .reshape(local_blocks, block_out, tok_count)
            )

        def first(weights, rows_of):
            return jnp.einsum("jki,kir->kjr", weights, rows_of, preferred_element_type=jnp.float32)

        act = mix(first(factors[0], tok_all))
        tan = mix(first(factors[1], tok_all))
        grad = mix(first(factors[2], goal_all) * weight)
    hess_mixed, back = mixed_stage(
        loaders, act, tan, grad, second_factor_blocks, second_factor_tangent
    )

    back = (
        back.reshape(local_blocks, all_blocks, pair, tok_count)
        .transpose(1, 0, 2, 3)
        .reshape(all_blocks, local_out, tok_count)
    )
    hess_first = jnp.einsum("kjr,kir->kij", back, tok_all, preferred_element_type=jnp.float32)
    in_share = block_in // loaders
    hess_first = hess_first.astype(jnp.bfloat16).reshape(
        all_blocks, loaders, in_share * local_out
    )
    hess_first = hess_first.transpose(1, 0, 2).reshape(
        loaders, features, local_blocks, in_share * local_out
    )
    hess_mixed, hess_first = reduce_stage(loaders, features, hess_mixed, hess_first)
    hess_first = (
        hess_first.reshape(features, local_blocks, in_share, local_out)
        .transpose(1, 2, 0, 3)
        .reshape(local_blocks, in_share, block_out)
    )
    return hess_first.astype(jnp.float32), hess_mixed


def solution(mesh):
    in_specs = (
        P("dp", "feat"),
        P("dp", "feat"),
        P("feat", None, None),
        P("feat", None, None),
        P("feat", None, None),
        P("feat", None, None),
        P("feat", None, None),
        P(),
        P(),
        P(),
    )
    out_specs = (P("feat", "dp", None), P("feat", "dp", None))
    return jax.shard_map(
        per_device, mesh=mesh, in_specs=in_specs, out_specs=out_specs, check_vma=False
    )
```

```python
import functools

import jax
import jax.numpy as jnp
import numpy as np
from jax import lax
from jax.experimental import pallas as pl
from jax.experimental.pallas import tpu as pltpu
from jax.sharding import PartitionSpec as P

inv_root_two = 0.7071067811865476
inv_root_two_pi = 0.3989422804014327
STEP = 2
MESH = pl.DeviceIdType.MESH


def column_loop(columns, body):
    tile = min(columns, 256)

    @pl.loop(0, columns // tile)
    def _(step):
        body(pl.ds(pl.multiple_of(step * tile, tile), tile))


def gather_kernel(loaders, features, fused, *refs):
    if fused:
        spread_ref, keep_ref, weight_ref = refs[4:7]
        from_hbm = refs[7:12]
        hess_out, back_out = refs[13:15]
        act_out, tan_out, grad_out = refs[15:18]
        share_refs = refs[18:21]
        mix_fac, mix_fac_tan = refs[21:23]
        local_sem = refs[23]
        refs = refs[:4] + (refs[24], refs[12]) + refs[25:]
    tok_ref, target_ref, send_sel_ref, take_sel_ref, fac_ref = refs[:5]
    tok_all, goal_all, fac_all, outgoing, arrived = refs[5:10]
    slot_send, slot_recv, fac_send, fac_recv, chip_send, chip_recv = refs[10:16]
    pair_send, pair_recv, line_send, line_recv = refs[16:]
    dev = lax.axis_index("dp")
    me = lax.axis_index("feat")
    columns = tok_ref.shape[1]
    slot = outgoing.shape[0] // loaders

    def to_dp(peer):
        return {"dp": peer}

    def to_feat(peer):
        return {"feat": peer}

    if fused:
        share = share_refs[0].shape[0]
        mine = pl.ds(pl.multiple_of(dev * share, share), share)
        moves = [
            pltpu.make_async_copy(src.at[mine] if n < 3 else src, dst, local_sem.at[n])
            for n, (src, dst) in enumerate(zip(from_hbm, share_refs + (mix_fac, mix_fac_tan)))
        ]
        for move in moves:
            move.start()
        for n in range(3):
            moves[n].wait()
            turned = share_refs[n][...].T
            out_rows = turned.shape[0] // features
            for f in range(features):
                fac_ref[f, n * out_rows : (n + 1) * out_rows] = turned[
                    f * out_rows : (f + 1) * out_rows
                ]

    barrier = pltpu.get_barrier_semaphore()
    for off in range(1, loaders):
        pl.semaphore_signal(
            barrier, inc=1, device_id=to_dp(lax.rem(dev + off, loaders)), device_id_type=MESH
        )
    for off in range(1, features):
        pl.semaphore_signal(
            barrier, inc=1, device_id=to_feat(lax.rem(me + off, features)), device_id_type=MESH
        )
    pl.semaphore_wait(barrier, loaders + features - 2)

    def remote(src, dst, send, recv, target):
        return pltpu.make_async_remote_copy(
            src_ref=src,
            dst_ref=dst,
            send_sem=send,
            recv_sem=recv,
            device_id=target,
            device_id_type=MESH,
        )

    fac_copies = []
    for off in range(1, features):
        peer = lax.rem(me + off, features)
        fac_copies.append(
            remote(
                fac_ref.at[peer],
                fac_all.at[dev, me],
                fac_send.at[off - 1],
                fac_recv.at[off - 1],
                to_feat(peer),
            )
        )
        fac_copies[-1].start()
    fac_all[dev, me] = fac_ref[me]

    def hop(ref, which, step, right):
        shard = jnp.maximum(me - step, 0) if right else jnp.minimum(me + step, features - 1)
        peer = jnp.minimum(me + 1, features - 1) if right else jnp.maximum(me - 1, 0)
        side = 0 if right else 1
        return remote(
            ref.at[shard],
            ref.at[shard],
            line_send.at[which, side, step],
            line_recv.at[which, side, step],
            to_feat(peer),
        )

    def has(step, right):
        return (me >= step) if right else (me + step <= features - 1)

    def sends(step, right):
        return has(step, right) & ((me < features - 1) if right else (me > 0))

    def line_step(ref, which, step):
        for right in (True, False):
            if step > 0:

                @pl.when(has(step, right))
                def _():
                    hop(ref, which, step - 1, right).wait_recv()

            if step < features - 1:

                @pl.when(sends(step, right))
                def _():
                    hop(ref, which, step, right).start()

    def line_end(ref, which):
        for step in range(features - 1):
            for right in (True, False):

                @pl.when(sends(step, right))
                def _():
                    hop(ref, which, step, right).wait_send()

    def turn_tokens(cols):
        tok_all[me, cols, :] = tok_ref[:, cols].T

    column_loop(columns, turn_tokens)
    line_step(tok_all, 0, 0)

    def pick(cols):
        outgoing[:, cols] = jnp.dot(
            send_sel_ref[...], target_ref[:, cols], preferred_element_type=jnp.float32
        ).astype(jnp.bfloat16)

    column_loop(columns, pick)
    slot_copies = []
    for off in range(1, loaders):
        peer = lax.rem(dev + off, loaders)
        slot_copies.append(
            remote(
                outgoing.at[pl.ds(pl.multiple_of(peer * slot, slot), slot)],
                arrived.at[pl.ds(pl.multiple_of(dev * slot, slot), slot)],
                slot_send.at[off - 1],
                slot_recv.at[off - 1],
                to_dp(peer),
            )
        )
        slot_copies[-1].start()
    own = pl.ds(pl.multiple_of(dev * slot, slot), slot)
    arrived[own] = outgoing[own]

    for copy in fac_copies:
        copy.wait_recv()
    chips = loaders // 2
    chip = dev // 2
    core = lax.rem(dev, 2)
    sibling = dev + 1 - 2 * core

    def to_pair(index, piece):
        return remote(
            fac_all.at[piece],
            fac_all.at[piece],
            pair_send.at[index],
            pair_recv.at[index],
            to_dp(sibling),
        )

    pair_copies = [to_pair(0, dev)]
    pair_copies[0].start()
    chip_copies = []
    for off in range(1, chips):
        peer = lax.rem(chip + off, chips) * 2 + core
        chip_copies.append(
            remote(
                fac_all.at[dev],
                fac_all.at[dev],
                chip_send.at[off - 1],
                chip_recv.at[off - 1],
                to_dp(peer),
            )
        )
        chip_copies[-1].start()

    if features > 2:
        line_step(tok_all, 0, 1)
    for copy in slot_copies:
        copy.wait_recv()

    def take(cols):
        goal_all[me, cols, :] = lax.dot_general(
            arrived[:, cols],
            take_sel_ref[...],
            (((0,), (0,)), ((), ())),
            preferred_element_type=jnp.float32,
        ).astype(jnp.bfloat16)

    column_loop(columns, take)
    line_step(goal_all, 1, 0)
    for step in range(2, features - 1):
        line_step(tok_all, 0, step)
    for off in range(1, chips):
        chip_copies[off - 1].wait_recv()
        piece = lax.rem(chip + chips - off, chips) * 2 + core
        pair_copies.append(to_pair(off, piece))
        pair_copies[-1].start()
    line_step(goal_all, 1, 1)
    line_step(tok_all, 0, features - 1)
    for copy in pair_copies:
        copy.wait()

    def first_stage(src, uses, lo, hi, near, far):
        if not fused:
            return
        per_shard, pieces = fused
        tall, wide = keep_ref.shape
        width = tall // act_out.shape[0]
        out_rows = spread_ref.shape[1]

        @pl.loop(lo * per_shard, hi * per_shard)
        def _(unit):
            shard = unit // per_shard
            part = unit % per_shard
            distance = jnp.maximum(shard - me, me - shard)

            @pl.when((distance >= near) & (distance <= far))
            def _():
                cols = src[shard, pl.ds(pl.multiple_of(part * wide, wide), wide), :]
                for which, out in uses:
                    rows = slice(which * out_rows, (which + 1) * out_rows)
                    compact = jnp.concatenate(
                        [fac_all[part * pieces + n, shard, rows, :] for n in range(pieces)], axis=1
                    )
                    spread = jnp.dot(
                        spread_ref[...], compact, preferred_element_type=jnp.float32
                    ).astype(jnp.bfloat16)
                    value = jnp.dot(
                        spread * keep_ref[...], cols, preferred_element_type=jnp.float32
                    )
                    if which == 2:
                        value = value * weight_ref[...]
                    place = pl.ds(pl.multiple_of(unit * width, width), width)
                    out[:, place, :] = value.reshape(out.shape[0], width, out.shape[2]).astype(
                        out.dtype
                    )

    if fused:
        on_tok = ((0, act_out), (1, tan_out))
        on_goal = ((2, grad_out),)
    else:
        on_tok = on_goal = ()
    half = features // 2
    first_stage(tok_all, on_tok, 0, half, 0, features)
    for step in range(2, features - 1):
        line_step(goal_all, 1, step)
    first_stage(tok_all, on_tok, half, features, 0, features)
    first_stage(goal_all, on_goal, 0, features, 0, features - 2)
    line_step(goal_all, 1, features - 1)
    first_stage(goal_all, on_goal, 0, features, features - 1, features)
    if fused:
        for move in moves[3:]:
            move.wait()
        parts, _, out_share, width = hess_out.shape

        @pl.loop(0, act_out.shape[0])
        def _(g):
            hess, back = mixed_block(
                act_out[g], tan_out[g], grad_out[g], mix_fac[g], mix_fac_tan[g]
            )
            hess_out[:, g] = hess.reshape(parts, out_share, width).astype(hess_out.dtype)
            back_out[g] = back.astype(back_out.dtype)

    for copy in slot_copies + fac_copies + chip_copies:
        copy.wait_send()
    line_end(tok_all, 0)
    line_end(goal_all, 1)


def gather_stage(loaders, features, operands, fused):
    tokens, _, send_sel, _ = operands[:4]
    rows, columns = tokens.shape
    slots = send_sel.shape[0]
    dma = pltpu.SemaphoreType.DMA
    vmem = pl.BlockSpec(memory_space=pltpu.VMEM)
    in_specs = [vmem] * len(operands)
    shards = jax.ShapeDtypeStruct((features, columns, rows), jnp.bfloat16)
    held = []
    if fused:
        in_specs[7:] = [pl.BlockSpec(memory_space=pl.ANY)] * 5
        in_rows, width = operands[7].shape
        share = in_rows // loaders
        blocks = operands[10].shape[0]
        pieces = (features, 3 * width // features, share)
        mixed = (blocks, width, rows)
        out_shape = [
            shards,
            jax.ShapeDtypeStruct((loaders, blocks, width // loaders, width), jnp.bfloat16),
            jax.ShapeDtypeStruct(mixed, jnp.bfloat16),
        ]
        shapes = [mixed] * 3 + [(share, width)] * 3 + [operands[10].shape] * 2
        held = [pltpu.VMEM(shape, jnp.bfloat16) for shape in shapes]
        held += [dma((5,))]
        shapes = [pieces, shards.shape, (loaders,) + pieces]
        held += [pltpu.VMEM(shape, jnp.bfloat16) for shape in shapes]
    else:
        pieces = jax.ShapeDtypeStruct((loaders,) + operands[4].shape, jnp.bfloat16)
        out_shape = [shards, shards, pieces]
    return pl.pallas_call(
        functools.partial(gather_kernel, loaders, features, fused),
        in_specs=in_specs,
        out_specs=[vmem] * len(out_shape),
        out_shape=out_shape,
        scratch_shapes=held
        + [
            pltpu.VMEM((slots, columns), jnp.bfloat16),
            pltpu.VMEM((slots, columns), jnp.bfloat16),
            dma((loaders - 1,)),
            dma((loaders - 1,)),
            dma((features - 1,)),
            dma((features - 1,)),
            dma((loaders // 2 - 1,)),
            dma((loaders // 2 - 1,)),
            dma((loaders // 2,)),
            dma((loaders // 2,)),
            dma((2, 2, features - 1)),
            dma((2, 2, features - 1)),
        ],
        compiler_params=pltpu.CompilerParams(
            collective_id=0, has_side_effects=True, vmem_limit_bytes=48 * 1024 * 1024
        ),
    )(*operands)


def reduce_kernel(
    loaders,
    features,
    mix_ref,
    fir_ref,
    mix_out,
    fir_out,
    mix_pair,
    fir_pair,
    mix_sum,
    fir_sum,
    mix_got,
    fir_got,
    fir_total,
    pair_send,
    pair_recv,
    chip_send,
    chip_recv,
    feat_send,
    feat_recv,
):
    dev = lax.axis_index("dp")
    me = lax.axis_index("feat")
    chips = loaders // 2
    chip = dev // 2
    core = lax.rem(dev, 2)
    sibling = dev + 1 - 2 * core

    def chip_at(off):
        return lax.rem(chip + off, chips)

    targets = [{"dp": sibling}]
    targets += [{"dp": chip_at(off) * 2 + core} for off in range(1, chips)]
    targets += [{"feat": lax.rem(me + off, features)} for off in range(1, features)]
    barrier = pltpu.get_barrier_semaphore()
    for target in targets:
        pl.semaphore_signal(barrier, inc=1, device_id=target, device_id_type=MESH)
    pl.semaphore_wait(barrier, len(targets))

    def remote(src, dst, send, recv, target):
        return pltpu.make_async_remote_copy(
            src_ref=src,
            dst_ref=dst,
            send_sem=send,
            recv_sem=recv,
            device_id=target,
            device_id_type=MESH,
        )

    parts = ((fir_ref, fir_pair, fir_sum, fir_got), (mix_ref, mix_pair, mix_sum, mix_got))
    order = list(range(1, chips)) + [0]
    pairs = {}
    for which, (ref, pair, _, _) in enumerate(parts):
        for off in order:
            there = chip_at(off)
            pairs[which, off] = remote(
                ref.at[there * 2 + 1 - core],
                pair.at[there],
                pair_send.at[which, off],
                pair_recv.at[which, off],
                {"dp": sibling},
            )
            pairs[which, off].start()

    def each(count, body):
        @pl.loop(0, count)
        def _(index):
            body(index)

    sent = {}
    for which, (ref, pair, total, got) in enumerate(parts):
        for off in range(1, chips):
            there = chip_at(off)
            pairs[which, off].wait_recv()

            def add(index):
                total[there, index] = (
                    ref[there * 2 + core, index].astype(jnp.float32)
                    + pair[there, index].astype(jnp.float32)
                ).astype(jnp.bfloat16)

            each(ref.shape[1], add)
            sent[which, off] = remote(
                total.at[there],
                got.at[off - 1],
                chip_send.at[which, off - 1],
                chip_recv.at[which, off - 1],
                {"dp": there * 2 + core},
            )
            sent[which, off].start()

    def finish(which, store):
        ref, pair, _, got = parts[which]
        pairs[which, 0].wait_recv()
        for off in range(1, chips):
            sent[which, off].wait_recv()

        def add(index):
            value = ref[dev, index].astype(jnp.float32) + pair[chip, index].astype(jnp.float32)
            for off in range(1, chips):
                value = value + got[off - 1, index].astype(jnp.float32)
            store(index, value)

        each(ref.shape[1], add)

    def store_first(index, value):
        fir_total[index] = value.astype(jnp.bfloat16)

    def store_mixed(index, value):
        mix_out[index] = value

    finish(0, store_first)
    last = []
    for off in range(1, features):
        peer = lax.rem(me + off, features)
        last.append(
            remote(
                fir_total.at[peer],
                fir_out.at[me],
                feat_send.at[off - 1],
                feat_recv.at[off - 1],
                {"feat": peer},
            )
        )
        last[-1].start()
    fir_out[me] = fir_total[me]
    finish(1, store_mixed)
    for copy in last:
        copy.wait()
    for copy in list(pairs.values()) + list(sent.values()):
        copy.wait_send()


def reduce_stage(loaders, features, mixed, first):
    chips = loaders // 2
    dma = pltpu.SemaphoreType.DMA
    vmem = pl.BlockSpec(memory_space=pltpu.VMEM)

    def buffers(count):
        return [pltpu.VMEM((count,) + a.shape[1:], jnp.bfloat16) for a in (mixed, first)]

    return pl.pallas_call(
        functools.partial(reduce_kernel, loaders, features),
        in_specs=[vmem] * 2,
        out_specs=[vmem] * 2,
        out_shape=[
            jax.ShapeDtypeStruct(mixed.shape[1:], jnp.float32),
            jax.ShapeDtypeStruct(first.shape[1:], jnp.bfloat16),
        ],
        scratch_shapes=buffers(chips)
        + buffers(chips)
        + buffers(chips - 1)
        + [
            pltpu.VMEM(first.shape[1:], jnp.bfloat16),
            dma((2, chips)),
            dma((2, chips)),
            dma((2, chips - 1)),
            dma((2, chips - 1)),
            dma((features - 1,)),
            dma((features - 1,)),
        ],
        compiler_params=pltpu.CompilerParams(
            collective_id=1, has_side_effects=True, vmem_limit_bytes=48 * 1024 * 1024
        ),
    )(mixed, first)


def mixed_block(act, tan, grad, fac, fac_tan):
    rows = act.shape[1]
    first_dims = (((0,), (0,)), ((), ()))
    both = lax.dot_general(
        fac,
        jnp.concatenate([act, tan], axis=1),
        first_dims,
        preferred_element_type=jnp.float32,
    )
    pre_act = both[:, :rows]
    pre_tan = both[:, rows:] + lax.dot_general(
        fac_tan, act, first_dims, preferred_element_type=jnp.float32
    )
    grad = grad.astype(jnp.float32)
    density = jnp.exp(-0.5 * pre_act * pre_act) * inv_root_two_pi
    cdf = 0.5 * (1.0 + lax.erf(pre_act * inv_root_two))
    pre_grad = (grad * (cdf + pre_act * density)).astype(jnp.bfloat16)
    pre_tan_grad = (grad * (density * (2.0 - pre_act * pre_act)) * pre_tan).astype(jnp.bfloat16)
    hess = lax.dot_general(
        jnp.concatenate([tan, act], axis=1),
        jnp.concatenate([pre_grad, pre_tan_grad], axis=1),
        (((1,), (1,)), ((), ())),
        preferred_element_type=jnp.float32,
    )
    back = jnp.dot(fac, pre_tan_grad, preferred_element_type=jnp.float32) + jnp.dot(
        fac_tan, pre_grad, preferred_element_type=jnp.float32
    )
    return hess, back


def mixed_kernel(act_ref, tan_ref, grad_ref, fac_ref, fac_tan_ref, hess_ref, back_ref):
    parts, _, share, width = hess_ref.shape
    for b in range(act_ref.shape[0]):
        hess, back = mixed_block(act_ref[b], tan_ref[b], grad_ref[b], fac_ref[b], fac_tan_ref[b])
        hess_ref[:, b] = hess.reshape(parts, share, width).astype(hess_ref.dtype)
        back_ref[b] = back.astype(back_ref.dtype)


def mixed_stage(loaders, act, tan, grad, fac, fac_tan):
    blocks, width, rows = act.shape
    thin = pl.BlockSpec((STEP, width, rows), lambda s: (s, 0, 0))
    wide = pl.BlockSpec((STEP, width, width), lambda s: (s, 0, 0))
    share = width // loaders
    split = pl.BlockSpec((loaders, STEP, share, width), lambda s: (0, s, 0, 0))
    return pl.pallas_call(
        mixed_kernel,
        grid=(blocks // STEP,),
        in_specs=[thin, thin, thin, wide, wide],
        out_specs=[split, thin],
        out_shape=[
            jax.ShapeDtypeStruct((loaders, blocks, share, width), jnp.bfloat16),
            jax.ShapeDtypeStruct((blocks, width, rows), jnp.bfloat16),
        ],
        compiler_params=pltpu.CompilerParams(vmem_limit_bytes=32 * 1024 * 1024),
        cost_estimate=pl.CostEstimate(
            flops=14 * blocks * width * width * rows,
            bytes_accessed=blocks * width * (6 * width + 8 * rows),
            transcendentals=2 * blocks * width * rows,
        ),
    )(act, tan, grad, fac, fac_tan)


def per_device(
    tokens,
    targets,
    first_blocks,
    second_factor_blocks,
    down_blocks,
    first_tangent,
    second_factor_tangent,
    doc_lengths,
    doc_owners,
    pack_offsets,
):
    loaders = lax.axis_size("dp")
    features = lax.axis_size("feat")
    device = lax.axis_index("dp")
    tok_count, feature_cols = tokens.shape
    pack_rows = targets.shape[0]
    slot_rows = -(-2 * tok_count // (16 * loaders)) * 16
    local_blocks, block_in, block_out = first_blocks.shape
    all_blocks = local_blocks * features
    local_out = block_out // features
    pair = local_out // local_blocks

    position = jnp.arange(slot_rows, dtype=jnp.int32)
    mine = (doc_owners == device).astype(jnp.int32)
    slot_start = jnp.sum(mine * pack_offsets, axis=1)
    pack_source = (slot_start[:, None] + position[None, :]).reshape(-1)
    send_sel = (
        pack_source[:, None] == jnp.arange(pack_rows, dtype=jnp.int32)[None, :]
    ).astype(jnp.bfloat16)
    my_lengths = lax.dynamic_index_in_dim(doc_lengths, device, 0, keepdims=False)
    my_owners = lax.dynamic_index_in_dim(doc_owners, device, 0, keepdims=False)
    my_starts = jnp.cumsum(my_lengths) - my_lengths
    row = jnp.arange(tok_count, dtype=jnp.int32)
    inside = (row[:, None] >= my_starts[None, :]) & (
        row[:, None] < (my_starts + my_lengths)[None, :]
    )
    inside_int = inside.astype(jnp.int32)
    source = jnp.sum(inside_int * (my_owners * slot_rows - my_starts)[None, :], axis=1) + row
    weight = jnp.sum(inside.astype(jnp.float32) / my_lengths.astype(jnp.float32)[None, :], axis=1)
    take_sel = (
        jnp.arange(loaders * slot_rows, dtype=jnp.int32)[:, None] == source[None, :]
    ).astype(jnp.bfloat16)

    rows = local_blocks * block_in
    share = rows // loaders
    stacked = [
        w.reshape(rows, block_out)
        for w in (first_blocks, first_tangent, jnp.swapaxes(down_blocks, 1, 2))
    ]

    group = 16 // pair
    wide = group * block_in
    whole_pieces = share % block_in == 0 and wide % share == 0 and local_blocks % group == 0
    fused = (local_blocks // group, wide // share) if whole_pieces else None
    operands = (tokens, targets, send_sel, take_sel)
    if fused:
        out_row = np.arange(16 * local_blocks)
        column = (out_row // 16) * pair + out_row % pair
        spread = column[:, None] == np.arange(local_out)[None, :]
        keep = ((out_row % 16) // pair)[:, None] == (np.arange(wide) // block_in)[None, :]
        operands += (
            jnp.asarray(spread, jnp.bfloat16),
            jnp.asarray(keep, jnp.bfloat16),
            weight[None, :],
            *stacked,
            second_factor_blocks,
            second_factor_tangent,
        )
        tok_all, hess_mixed, back = gather_stage(loaders, features, operands, fused)
        tok_all = tok_all.reshape(all_blocks, block_in, tok_count)
    else:
        factors = jnp.stack(
            [lax.dynamic_slice_in_dim(w, device * share, share, 0) for w in stacked]
        )
        factors = factors.reshape(3, share, features, local_out).transpose(2, 0, 3, 1)
        factors = factors.reshape(features, 3 * local_out, share)
        tok_all, goal_all, factors = gather_stage(loaders, features, operands + (factors,), None)
        factors = factors.reshape(loaders, features, 3, local_out, share)
        factors = factors.transpose(2, 3, 1, 0, 4).reshape(3, local_out, all_blocks, block_in)
        tok_all = tok_all.reshape(all_blocks, block_in, tok_count)
        goal_all = goal_all.reshape(all_blocks, block_in, tok_count)

        def mix(values):
            return (
                values.astype(jnp.bfloat16)
                .reshape(all_blocks, local_blocks, pair, tok_count)
                .transpose(1, 0, 2, 3)
                .reshape(local_blocks, block_out, tok_count)
            )

        def first(weights, rows_of):
            return jnp.einsum("jki,kir->kjr", weights, rows_of, preferred_element_type=jnp.float32)

        act = mix(first(factors[0], tok_all))
        tan = mix(first(factors[1], tok_all))
        grad = mix(first(factors[2], goal_all) * weight)
        hess_mixed, back = mixed_stage(
            loaders, act, tan, grad, second_factor_blocks, second_factor_tangent
        )

    back = (
        back.reshape(local_blocks, all_blocks, pair, tok_count)
        .transpose(1, 0, 2, 3)
        .reshape(all_blocks, local_out, tok_count)
    )
    hess_first = jnp.einsum("kjr,kir->kij", back, tok_all, preferred_element_type=jnp.float32)
    in_share = block_in // loaders
    hess_first = hess_first.astype(jnp.bfloat16).reshape(
        all_blocks, loaders, in_share * local_out
    )
    hess_first = hess_first.transpose(1, 0, 2).reshape(
        loaders, features, local_blocks, in_share * local_out
    )
    hess_mixed, hess_first = reduce_stage(loaders, features, hess_mixed, hess_first)
    hess_first = (
        hess_first.reshape(features, local_blocks, in_share, local_out)
        .transpose(1, 2, 0, 3)
        .reshape(local_blocks, in_share, block_out)
    )
    return hess_first.astype(jnp.float32), hess_mixed


def solution(mesh):
    in_specs = (
        P("dp", "feat"),
        P("dp", "feat"),
        P("feat", None, None),
        P("feat", None, None),
        P("feat", None, None),
        P("feat", None, None),
        P("feat", None, None),
        P(),
        P(),
        P(),
    )
    out_specs = (P("feat", "dp", None), P("feat", "dp", None))
    return jax.shard_map(
        per_device, mesh=mesh, in_specs=in_specs, out_specs=out_specs, check_vma=False
    )
```

```python
import functools

import jax
import jax.numpy as jnp
import numpy as np
from jax import lax
from jax.experimental import pallas as pl
from jax.experimental.pallas import tpu as pltpu
from jax.sharding import PartitionSpec as P

inv_root_two = 0.7071067811865476
inv_root_two_pi = 0.3989422804014327
STEP = 2
MESH = pl.DeviceIdType.MESH


def column_loop(columns, body):
    tile = min(columns, 256)

    @pl.loop(0, columns // tile)
    def _(step):
        body(pl.ds(pl.multiple_of(step * tile, tile), tile))


def gather_kernel(loaders, features, fused, *refs):
    if fused:
        spread_ref, keep_ref, weight_ref = refs[4:7]
        from_hbm = refs[7:12]
        hess_out, back_out = refs[13:15]
        act_out, tan_out, grad_out = refs[15:18]
        share_refs = refs[18:21]
        mix_fac, mix_fac_tan = refs[21:23]
        local_sem = refs[23]
        refs = refs[:4] + (refs[24], refs[12]) + refs[25:]
    tok_ref, target_ref, send_sel_ref, take_sel_ref, fac_ref = refs[:5]
    tok_all, goal_all, fac_all, outgoing, arrived = refs[5:10]
    slot_send, slot_recv, fac_send, fac_recv, chip_send, chip_recv = refs[10:16]
    pair_send, pair_recv, line_send, line_recv = refs[16:]
    dev = lax.axis_index("dp")
    me = lax.axis_index("feat")
    columns = tok_ref.shape[1]
    slot = outgoing.shape[0] // loaders

    def to_dp(peer):
        return {"dp": peer}

    def to_feat(peer):
        return {"feat": peer}

    if fused:
        share = share_refs[0].shape[0]
        mine = pl.ds(pl.multiple_of(dev * share, share), share)
        moves = [
            pltpu.make_async_copy(src.at[mine] if n < 3 else src, dst, local_sem.at[n])
            for n, (src, dst) in enumerate(zip(from_hbm, share_refs + (mix_fac, mix_fac_tan)))
        ]
        for move in moves:
            move.start()
        for n in range(3):
            moves[n].wait()
            turned = share_refs[n][...].T
            out_rows = turned.shape[0] // features
            for f in range(features):
                fac_ref[f, n * out_rows : (n + 1) * out_rows] = turned[
                    f * out_rows : (f + 1) * out_rows
                ]

    barrier = pltpu.get_barrier_semaphore()
    for off in range(1, loaders):
        pl.semaphore_signal(
            barrier, inc=1, device_id=to_dp(lax.rem(dev + off, loaders)), device_id_type=MESH
        )
    for off in range(1, features):
        pl.semaphore_signal(
            barrier, inc=1, device_id=to_feat(lax.rem(me + off, features)), device_id_type=MESH
        )
    pl.semaphore_wait(barrier, loaders + features - 2)

    def remote(src, dst, send, recv, target):
        return pltpu.make_async_remote_copy(
            src_ref=src,
            dst_ref=dst,
            send_sem=send,
            recv_sem=recv,
            device_id=target,
            device_id_type=MESH,
        )

    fac_copies = []
    for off in range(1, features):
        peer = lax.rem(me + off, features)
        fac_copies.append(
            remote(
                fac_ref.at[peer],
                fac_all.at[dev, me],
                fac_send.at[off - 1],
                fac_recv.at[off - 1],
                to_feat(peer),
            )
        )
        fac_copies[-1].start()
    fac_all[dev, me] = fac_ref[me]

    def hop(ref, which, step, right):
        shard = jnp.maximum(me - step, 0) if right else jnp.minimum(me + step, features - 1)
        peer = jnp.minimum(me + 1, features - 1) if right else jnp.maximum(me - 1, 0)
        side = 0 if right else 1
        return remote(
            ref.at[shard],
            ref.at[shard],
            line_send.at[which, side, step],
            line_recv.at[which, side, step],
            to_feat(peer),
        )

    def has(step, right):
        return (me >= step) if right else (me + step <= features - 1)

    def sends(step, right):
        return has(step, right) & ((me < features - 1) if right else (me > 0))

    def line_step(ref, which, step):
        for right in (True, False):
            if step > 0:

                @pl.when(has(step, right))
                def _():
                    hop(ref, which, step - 1, right).wait_recv()

            if step < features - 1:

                @pl.when(sends(step, right))
                def _():
                    hop(ref, which, step, right).start()

    def line_end(ref, which):
        for step in range(features - 1):
            for right in (True, False):

                @pl.when(sends(step, right))
                def _():
                    hop(ref, which, step, right).wait_send()

    def turn_tokens(cols):
        tok_all[me, cols, :] = tok_ref[:, cols].T

    column_loop(columns, turn_tokens)
    line_step(tok_all, 0, 0)

    def pick(cols):
        outgoing[:, cols] = jnp.dot(
            send_sel_ref[...], target_ref[:, cols], preferred_element_type=jnp.float32
        ).astype(jnp.bfloat16)

    column_loop(columns, pick)
    slot_copies = []
    for off in range(1, loaders):
        peer = lax.rem(dev + off, loaders)
        slot_copies.append(
            remote(
                outgoing.at[pl.ds(pl.multiple_of(peer * slot, slot), slot)],
                arrived.at[pl.ds(pl.multiple_of(dev * slot, slot), slot)],
                slot_send.at[off - 1],
                slot_recv.at[off - 1],
                to_dp(peer),
            )
        )
        slot_copies[-1].start()
    own = pl.ds(pl.multiple_of(dev * slot, slot), slot)
    arrived[own] = outgoing[own]

    for copy in fac_copies:
        copy.wait_recv()
    chips = loaders // 2
    chip = dev // 2
    core = lax.rem(dev, 2)
    sibling = dev + 1 - 2 * core

    def to_pair(index, piece):
        return remote(
            fac_all.at[piece],
            fac_all.at[piece],
            pair_send.at[index],
            pair_recv.at[index],
            to_dp(sibling),
        )

    pair_copies = [to_pair(0, dev)]
    pair_copies[0].start()
    chip_copies = []
    for off in range(1, chips):
        peer = lax.rem(chip + off, chips) * 2 + core
        chip_copies.append(
            remote(
                fac_all.at[dev],
                fac_all.at[dev],
                chip_send.at[off - 1],
                chip_recv.at[off - 1],
                to_dp(peer),
            )
        )
        chip_copies[-1].start()

    if features > 2:
        line_step(tok_all, 0, 1)
    for copy in slot_copies:
        copy.wait_recv()

    def take(cols):
        goal_all[me, cols, :] = lax.dot_general(
            arrived[:, cols],
            take_sel_ref[...],
            (((0,), (0,)), ((), ())),
            preferred_element_type=jnp.float32,
        ).astype(jnp.bfloat16)

    column_loop(columns, take)
    line_step(goal_all, 1, 0)
    for step in range(2, features - 1):
        line_step(tok_all, 0, step)
    for off in range(1, chips):
        chip_copies[off - 1].wait_recv()
        piece = lax.rem(chip + chips - off, chips) * 2 + core
        pair_copies.append(to_pair(off, piece))
        pair_copies[-1].start()
    line_step(goal_all, 1, 1)
    line_step(tok_all, 0, features - 1)
    for copy in pair_copies:
        copy.wait()

    def first_stage(src, uses, lo, hi, near, far):
        if not fused:
            return
        per_shard, pieces = fused
        tall, wide = keep_ref.shape
        width = tall // act_out.shape[0]
        out_rows = spread_ref.shape[1]

        @pl.loop(lo * per_shard, hi * per_shard)
        def _(unit):
            shard = unit // per_shard
            part = unit % per_shard
            distance = jnp.maximum(shard - me, me - shard)

            @pl.when((distance >= near) & (distance <= far))
            def _():
                cols = src[shard, pl.ds(pl.multiple_of(part * wide, wide), wide), :]
                for which, out in uses:
                    rows = slice(which * out_rows, (which + 1) * out_rows)
                    compact = jnp.concatenate(
                        [fac_all[part * pieces + n, shard, rows, :] for n in range(pieces)], axis=1
                    )
                    spread = jnp.dot(
                        spread_ref[...], compact, preferred_element_type=jnp.float32
                    ).astype(jnp.bfloat16)
                    value = jnp.dot(
                        spread * keep_ref[...], cols, preferred_element_type=jnp.float32
                    )
                    if which == 2:
                        value = value * weight_ref[...]
                    place = pl.ds(pl.multiple_of(unit * width, width), width)
                    out[:, place, :] = value.reshape(out.shape[0], width, out.shape[2]).astype(
                        out.dtype
                    )

    if fused:
        on_tok = ((0, act_out), (1, tan_out))
        on_goal = ((2, grad_out),)
    else:
        on_tok = on_goal = ()
    half = features // 2
    first_stage(tok_all, on_tok, 0, half, 0, features)
    for step in range(2, features - 1):
        line_step(goal_all, 1, step)
    first_stage(tok_all, on_tok, half, features, 0, features)
    first_stage(goal_all, on_goal, 0, features, 0, features - 2)
    line_step(goal_all, 1, features - 1)
    first_stage(goal_all, on_goal, 0, features, features - 1, features)
    if fused:
        for move in moves[3:]:
            move.wait()
        parts, _, out_share, width = hess_out.shape

        @pl.loop(0, act_out.shape[0])
        def _(g):
            hess, back = mixed_block(
                act_out[g], tan_out[g], grad_out[g], mix_fac[g], mix_fac_tan[g]
            )
            hess_out[:, g] = hess.reshape(parts, out_share, width).astype(hess_out.dtype)
            back_out[g] = back.astype(back_out.dtype)

    for copy in slot_copies + fac_copies + chip_copies:
        copy.wait_send()
    line_end(tok_all, 0)
    line_end(goal_all, 1)


def gather_stage(loaders, features, operands, fused):
    tokens, _, send_sel, _ = operands[:4]
    rows, columns = tokens.shape
    slots = send_sel.shape[0]
    dma = pltpu.SemaphoreType.DMA
    vmem = pl.BlockSpec(memory_space=pltpu.VMEM)
    in_specs = [vmem] * len(operands)
    shards = jax.ShapeDtypeStruct((features, columns, rows), jnp.bfloat16)
    held = []
    if fused:
        in_specs[7:] = [pl.BlockSpec(memory_space=pl.ANY)] * 5
        in_rows, width = operands[7].shape
        share = in_rows // loaders
        blocks = operands[10].shape[0]
        pieces = (features, 3 * width // features, share)
        mixed = (blocks, width, rows)
        out_shape = [
            shards,
            jax.ShapeDtypeStruct((loaders, blocks, width // loaders, width), jnp.bfloat16),
            jax.ShapeDtypeStruct(mixed, jnp.bfloat16),
        ]
        shapes = [mixed] * 3 + [(share, width)] * 3 + [operands[10].shape] * 2
        held = [pltpu.VMEM(shape, jnp.bfloat16) for shape in shapes]
        held += [dma((5,))]
        shapes = [pieces, shards.shape, (loaders,) + pieces]
        held += [pltpu.VMEM(shape, jnp.bfloat16) for shape in shapes]
    else:
        pieces = jax.ShapeDtypeStruct((loaders,) + operands[4].shape, jnp.bfloat16)
        out_shape = [shards, shards, pieces]
    return pl.pallas_call(
        functools.partial(gather_kernel, loaders, features, fused),
        in_specs=in_specs,
        out_specs=[vmem] * len(out_shape),
        out_shape=out_shape,
        scratch_shapes=held
        + [
            pltpu.VMEM((slots, columns), jnp.bfloat16),
            pltpu.VMEM((slots, columns), jnp.bfloat16),
            dma((loaders - 1,)),
            dma((loaders - 1,)),
            dma((features - 1,)),
            dma((features - 1,)),
            dma((loaders // 2 - 1,)),
            dma((loaders // 2 - 1,)),
            dma((loaders // 2,)),
            dma((loaders // 2,)),
            dma((2, 2, features - 1)),
            dma((2, 2, features - 1)),
        ],
        compiler_params=pltpu.CompilerParams(
            collective_id=0, has_side_effects=True, vmem_limit_bytes=60 * 1024 * 1024
        ),
    )(*operands)


def reduce_kernel(
    loaders,
    features,
    mix_ref,
    fir_ref,
    mix_out,
    fir_out,
    mix_pair,
    fir_pair,
    mix_sum,
    fir_sum,
    mix_got,
    fir_got,
    fir_total,
    pair_send,
    pair_recv,
    chip_send,
    chip_recv,
    feat_send,
    feat_recv,
):
    dev = lax.axis_index("dp")
    me = lax.axis_index("feat")
    chips = loaders // 2
    chip = dev // 2
    core = lax.rem(dev, 2)
    sibling = dev + 1 - 2 * core

    def chip_at(off):
        return lax.rem(chip + off, chips)

    targets = [{"dp": sibling}]
    targets += [{"dp": chip_at(off) * 2 + core} for off in range(1, chips)]
    targets += [{"feat": lax.rem(me + off, features)} for off in range(1, features)]
    barrier = pltpu.get_barrier_semaphore()
    for target in targets:
        pl.semaphore_signal(barrier, inc=1, device_id=target, device_id_type=MESH)
    pl.semaphore_wait(barrier, len(targets))

    def remote(src, dst, send, recv, target):
        return pltpu.make_async_remote_copy(
            src_ref=src,
            dst_ref=dst,
            send_sem=send,
            recv_sem=recv,
            device_id=target,
            device_id_type=MESH,
        )

    parts = ((fir_ref, fir_pair, fir_sum, fir_got), (mix_ref, mix_pair, mix_sum, mix_got))
    order = list(range(1, chips)) + [0]
    pairs = {}
    for which, (ref, pair, _, _) in enumerate(parts):
        for off in order:
            there = chip_at(off)
            pairs[which, off] = remote(
                ref.at[there * 2 + 1 - core],
                pair.at[there],
                pair_send.at[which, off],
                pair_recv.at[which, off],
                {"dp": sibling},
            )
            pairs[which, off].start()

    def each(count, body):
        @pl.loop(0, count)
        def _(index):
            body(index)

    sent = {}
    for which, (ref, pair, total, got) in enumerate(parts):
        for off in range(1, chips):
            there = chip_at(off)
            pairs[which, off].wait_recv()

            def add(index):
                total[there, index] = (
                    ref[there * 2 + core, index].astype(jnp.float32)
                    + pair[there, index].astype(jnp.float32)
                ).astype(jnp.bfloat16)

            each(ref.shape[1], add)
            sent[which, off] = remote(
                total.at[there],
                got.at[off - 1],
                chip_send.at[which, off - 1],
                chip_recv.at[which, off - 1],
                {"dp": there * 2 + core},
            )
            sent[which, off].start()

    def finish(which, store):
        ref, pair, _, got = parts[which]
        pairs[which, 0].wait_recv()
        for off in range(1, chips):
            sent[which, off].wait_recv()

        def add(index):
            value = ref[dev, index].astype(jnp.float32) + pair[chip, index].astype(jnp.float32)
            for off in range(1, chips):
                value = value + got[off - 1, index].astype(jnp.float32)
            store(index, value)

        each(ref.shape[1], add)

    def store_first(index, value):
        fir_total[index] = value.astype(jnp.bfloat16)

    def store_mixed(index, value):
        mix_out[index] = value

    finish(0, store_first)
    last = []
    for off in range(1, features):
        peer = lax.rem(me + off, features)
        last.append(
            remote(
                fir_total.at[peer],
                fir_out.at[me],
                feat_send.at[off - 1],
                feat_recv.at[off - 1],
                {"feat": peer},
            )
        )
        last[-1].start()
    fir_out[me] = fir_total[me]
    finish(1, store_mixed)
    for copy in last:
        copy.wait()
    for copy in list(pairs.values()) + list(sent.values()):
        copy.wait_send()


def reduce_stage(loaders, features, mixed, first):
    chips = loaders // 2
    dma = pltpu.SemaphoreType.DMA
    vmem = pl.BlockSpec(memory_space=pltpu.VMEM)

    def buffers(count):
        return [pltpu.VMEM((count,) + a.shape[1:], jnp.bfloat16) for a in (mixed, first)]

    return pl.pallas_call(
        functools.partial(reduce_kernel, loaders, features),
        in_specs=[vmem] * 2,
        out_specs=[vmem] * 2,
        out_shape=[
            jax.ShapeDtypeStruct(mixed.shape[1:], jnp.float32),
            jax.ShapeDtypeStruct(first.shape[1:], jnp.bfloat16),
        ],
        scratch_shapes=buffers(chips)
        + buffers(chips)
        + buffers(chips - 1)
        + [
            pltpu.VMEM(first.shape[1:], jnp.bfloat16),
            dma((2, chips)),
            dma((2, chips)),
            dma((2, chips - 1)),
            dma((2, chips - 1)),
            dma((features - 1,)),
            dma((features - 1,)),
        ],
        compiler_params=pltpu.CompilerParams(
            collective_id=1, has_side_effects=True, vmem_limit_bytes=48 * 1024 * 1024
        ),
    )(mixed, first)


def mixed_block(act, tan, grad, fac, fac_tan):
    rows = act.shape[1]
    first_dims = (((0,), (0,)), ((), ()))
    both = lax.dot_general(
        fac,
        jnp.concatenate([act, tan], axis=1),
        first_dims,
        preferred_element_type=jnp.float32,
    )
    pre_act = both[:, :rows]
    pre_tan = both[:, rows:] + lax.dot_general(
        fac_tan, act, first_dims, preferred_element_type=jnp.float32
    )
    grad = grad.astype(jnp.float32)
    density = jnp.exp(-0.5 * pre_act * pre_act) * inv_root_two_pi
    cdf = 0.5 * (1.0 + lax.erf(pre_act * inv_root_two))
    pre_grad = (grad * (cdf + pre_act * density)).astype(jnp.bfloat16)
    pre_tan_grad = (grad * (density * (2.0 - pre_act * pre_act)) * pre_tan).astype(jnp.bfloat16)
    hess = lax.dot_general(
        jnp.concatenate([tan, act], axis=1),
        jnp.concatenate([pre_grad, pre_tan_grad], axis=1),
        (((1,), (1,)), ((), ())),
        preferred_element_type=jnp.float32,
    )
    back = jnp.dot(fac, pre_tan_grad, preferred_element_type=jnp.float32) + jnp.dot(
        fac_tan, pre_grad, preferred_element_type=jnp.float32
    )
    return hess, back


def mixed_kernel(act_ref, tan_ref, grad_ref, fac_ref, fac_tan_ref, hess_ref, back_ref):
    parts, _, share, width = hess_ref.shape
    for b in range(act_ref.shape[0]):
        hess, back = mixed_block(act_ref[b], tan_ref[b], grad_ref[b], fac_ref[b], fac_tan_ref[b])
        hess_ref[:, b] = hess.reshape(parts, share, width).astype(hess_ref.dtype)
        back_ref[b] = back.astype(back_ref.dtype)


def mixed_stage(loaders, act, tan, grad, fac, fac_tan):
    blocks, width, rows = act.shape
    thin = pl.BlockSpec((STEP, width, rows), lambda s: (s, 0, 0))
    wide = pl.BlockSpec((STEP, width, width), lambda s: (s, 0, 0))
    share = width // loaders
    split = pl.BlockSpec((loaders, STEP, share, width), lambda s: (0, s, 0, 0))
    return pl.pallas_call(
        mixed_kernel,
        grid=(blocks // STEP,),
        in_specs=[thin, thin, thin, wide, wide],
        out_specs=[split, thin],
        out_shape=[
            jax.ShapeDtypeStruct((loaders, blocks, share, width), jnp.bfloat16),
            jax.ShapeDtypeStruct((blocks, width, rows), jnp.bfloat16),
        ],
        compiler_params=pltpu.CompilerParams(vmem_limit_bytes=32 * 1024 * 1024),
        cost_estimate=pl.CostEstimate(
            flops=14 * blocks * width * width * rows,
            bytes_accessed=blocks * width * (6 * width + 8 * rows),
            transcendentals=2 * blocks * width * rows,
        ),
    )(act, tan, grad, fac, fac_tan)


def per_device(
    tokens,
    targets,
    first_blocks,
    second_factor_blocks,
    down_blocks,
    first_tangent,
    second_factor_tangent,
    doc_lengths,
    doc_owners,
    pack_offsets,
):
    loaders = lax.axis_size("dp")
    features = lax.axis_size("feat")
    device = lax.axis_index("dp")
    tok_count, feature_cols = tokens.shape
    pack_rows = targets.shape[0]
    slot_rows = -(-2 * tok_count // (16 * loaders)) * 16
    local_blocks, block_in, block_out = first_blocks.shape
    all_blocks = local_blocks * features
    local_out = block_out // features
    pair = local_out // local_blocks

    position = jnp.arange(slot_rows, dtype=jnp.int32)
    mine = (doc_owners == device).astype(jnp.int32)
    slot_start = jnp.sum(mine * pack_offsets, axis=1)
    pack_source = (slot_start[:, None] + position[None, :]).reshape(-1)
    send_sel = (
        pack_source[:, None] == jnp.arange(pack_rows, dtype=jnp.int32)[None, :]
    ).astype(jnp.bfloat16)
    my_lengths = lax.dynamic_index_in_dim(doc_lengths, device, 0, keepdims=False)
    my_owners = lax.dynamic_index_in_dim(doc_owners, device, 0, keepdims=False)
    my_starts = jnp.cumsum(my_lengths) - my_lengths
    row = jnp.arange(tok_count, dtype=jnp.int32)
    inside = (row[:, None] >= my_starts[None, :]) & (
        row[:, None] < (my_starts + my_lengths)[None, :]
    )
    inside_int = inside.astype(jnp.int32)
    source = jnp.sum(inside_int * (my_owners * slot_rows - my_starts)[None, :], axis=1) + row
    weight = jnp.sum(inside.astype(jnp.float32) / my_lengths.astype(jnp.float32)[None, :], axis=1)
    take_sel = (
        jnp.arange(loaders * slot_rows, dtype=jnp.int32)[:, None] == source[None, :]
    ).astype(jnp.bfloat16)

    rows = local_blocks * block_in
    share = rows // loaders
    stacked = [
        w.reshape(rows, block_out)
        for w in (first_blocks, first_tangent, jnp.swapaxes(down_blocks, 1, 2))
    ]

    group = 16 // pair
    wide = group * block_in
    whole_pieces = share % block_in == 0 and wide % share == 0 and local_blocks % group == 0
    fused = (local_blocks // group, wide // share) if whole_pieces else None
    operands = (tokens, targets, send_sel, take_sel)
    if fused:
        out_row = np.arange(16 * local_blocks)
        column = (out_row // 16) * pair + out_row % pair
        spread = column[:, None] == np.arange(local_out)[None, :]
        keep = ((out_row % 16) // pair)[:, None] == (np.arange(wide) // block_in)[None, :]
        operands += (
            jnp.asarray(spread, jnp.bfloat16),
            jnp.asarray(keep, jnp.bfloat16),
            weight[None, :],
            *stacked,
            second_factor_blocks,
            second_factor_tangent,
        )
        tok_all, hess_mixed, back = gather_stage(loaders, features, operands, fused)
        tok_all = tok_all.reshape(all_blocks, block_in, tok_count)
    else:
        factors = jnp.stack(
            [lax.dynamic_slice_in_dim(w, device * share, share, 0) for w in stacked]
        )
        factors = factors.reshape(3, share, features, local_out).transpose(2, 0, 3, 1)
        factors = factors.reshape(features, 3 * local_out, share)
        tok_all, goal_all, factors = gather_stage(loaders, features, operands + (factors,), None)
        factors = factors.reshape(loaders, features, 3, local_out, share)
        factors = factors.transpose(2, 3, 1, 0, 4).reshape(3, local_out, all_blocks, block_in)
        tok_all = tok_all.reshape(all_blocks, block_in, tok_count)
        goal_all = goal_all.reshape(all_blocks, block_in, tok_count)

        def mix(values):
            return (
                values.astype(jnp.bfloat16)
                .reshape(all_blocks, local_blocks, pair, tok_count)
                .transpose(1, 0, 2, 3)
                .reshape(local_blocks, block_out, tok_count)
            )

        def first(weights, rows_of):
            return jnp.einsum("jki,kir->kjr", weights, rows_of, preferred_element_type=jnp.float32)

        act = mix(first(factors[0], tok_all))
        tan = mix(first(factors[1], tok_all))
        grad = mix(first(factors[2], goal_all) * weight)
        hess_mixed, back = mixed_stage(
            loaders, act, tan, grad, second_factor_blocks, second_factor_tangent
        )

    back = (
        back.reshape(local_blocks, all_blocks, pair, tok_count)
        .transpose(1, 0, 2, 3)
        .reshape(all_blocks, local_out, tok_count)
    )
    hess_first = jnp.einsum("kjr,kir->kij", back, tok_all, preferred_element_type=jnp.float32)
    in_share = block_in // loaders
    hess_first = hess_first.astype(jnp.bfloat16).reshape(
        all_blocks, loaders, in_share * local_out
    )
    hess_first = hess_first.transpose(1, 0, 2).reshape(
        loaders, features, local_blocks, in_share * local_out
    )
    hess_mixed, hess_first = reduce_stage(loaders, features, hess_mixed, hess_first)
    hess_first = (
        hess_first.reshape(features, local_blocks, in_share, local_out)
        .transpose(1, 2, 0, 3)
        .reshape(local_blocks, in_share, block_out)
    )
    return hess_first.astype(jnp.float32), hess_mixed


def solution(mesh):
    in_specs = (
        P("dp", "feat"),
        P("dp", "feat"),
        P("feat", None, None),
        P("feat", None, None),
        P("feat", None, None),
        P("feat", None, None),
        P("feat", None, None),
        P(),
        P(),
        P(),
    )
    out_specs = (P("feat", "dp", None), P("feat", "dp", None))
    return jax.shard_map(
        per_device, mesh=mesh, in_specs=in_specs, out_specs=out_specs, check_vma=False
    )
```
